256 devices in a mesh: dp: 16 (over y, x), rep: 16 (over z, core).
Axes of the slice: x: 4, y: 4, z: 8, core: 2. Of those that a mesh axis runs over, the one named last changes fastest.
Arguments:
- latent_query_rows: bfloat16 [2048, 64, 512], P(('rep', 'dp')), parts along dimension 0, may hold values from -32 to 32
- rotary_query_parts: bfloat16 [2048, 4096], P(('rep', 'dp')), parts along dimension 0, may hold values from -3 to 3
- latent_cache_rows: bfloat16 [2048, 256, 512], P(('rep', 'dp')), parts along dimension 0, may hold values from -4 to 4
- rotary_cache_keys: bfloat16 [2048, 64, 256], P(('rep', 'dp')), parts along dimension 0, may hold values from -6 to 6
- lengths: int32 [2048], P(('rep', 'dp')), parts along dimension 0, may hold values from 2 to 256, as said below
- adapters: int32 [2048], P(('rep', 'dp')), parts along dimension 0, may hold values from 0 to 63
- value_up_weight: bfloat16 [64, 512, 128], P('dp'), may hold values from -1.5 to 1.5
- output_weight: bfloat16 [8192, 7168], P('dp'), may hold values from -0.0625 to 0.0625
- down_factor_matrix: bfloat16 [8192, 1024], P('dp'), may hold values from -0.0625 to 0.0625
- up_factor_matrix: bfloat16 [16, 64, 7168], P('dp'), may hold values from -1.5 to 1.5
Outputs:
- attn_out: bfloat16 [2048, 7168], P(('rep', 'dp')), parts along dimension 0
The draws below stay inside these ranges and needn't reach their ends.
There are 16 independent parts, one for each index of `rep`. The reference program is written for one: setup_inputs(seed, part) draws one part's arguments, and reference() takes and returns one part's arrays. A program takes and returns all parts, laid end to end along the dimension named above; an argument that names none is the same for every part. Nothing has to cross between parts.
Inputs may be any that keep to these rules, and one draw needn't show every extreme that they name: `lengths`: live cache positions of a request.
All inputs are finite; a program needn't handle non-finite values.
Results may differ from the reference program's by a relative error of at most 0.018.
Values may be sent and summed in bfloat16 or wider, within the bound.
No kernel may reach another device: no remote copies, remote signals or barrier semaphores. Data moves between devices by JAX's collectives and lax.ppermute only.
A program may use at most 64 MiB of HBM per device.

```python
import math
import jax
import jax.numpy as jnp
import numpy as np

MODEL_WIDTH = 7168
LOCAL_HEADS = 64
LAT = 512
ROPE = 64
VALUE_WIDTH = 128
ADAPTER_RANK = 16
ADAPTER_COUNT = 64
CACHE = 256
REQ_DEV = 8
REQUEST_COUNT = 128


def shared_latent(key):
    return jnp.clip(jax.random.normal(key, (REQUEST_COUNT, CACHE, LAT), jnp.float32), -4.0, 4.0)


def draw_latent_cache_rows(key, part):
    base = shared_latent(key)
    return base.astype(jnp.bfloat16)


def draw_latent_query_rows(key, part):
    key = jax.random.fold_in(key, 12)
    return jnp.clip(0.5 * jax.random.normal(key, (REQUEST_COUNT, LOCAL_HEADS, LAT), jnp.float32), -3.0, 3.0).astype(jnp.bfloat16)


def draw_lengths(key, part):
    key = jax.random.fold_in(key, 13)
    level_key, spread_key, index_key = jax.random.split(key, 3)
    level = jax.random.randint(level_key, (REQUEST_COUNT // REQ_DEV,), 1, 5)
    level_rows = jnp.repeat(level, REQ_DEV, total_repeat_length=REQUEST_COUNT)
    spread = jax.random.randint(spread_key, (REQUEST_COUNT,), 0, CACHE - 1)
    result = 2 + spread * level_rows // 4
    longest = jax.random.randint(index_key, (), 0, REQUEST_COUNT)
    return jnp.where(jnp.arange(REQUEST_COUNT) == longest, CACHE, result).astype(jnp.int32)


def plant(values, key, low, largest):
    longest = values.shape.index(max(values.shape))
    spots = []
    for shift in (0, 1):
        where = [jax.random.randint(jax.random.fold_in(key, axis), (), 0, length) for axis, length in enumerate(values.shape)]
        where[longest] = (where[longest] + shift) % values.shape[longest]
        spots.append(tuple(where))
    return values.at[spots[0]].set(low).at[spots[1]].set(largest)


def levels(rng, extent, pieces, smallest, high):
    level, own = 1.0, jax.random.fold_in(rng, 6)
    for dim, shards_of in pieces:
        heights = jnp.exp(jax.random.uniform(jax.random.fold_in(own, dim), (shards_of,), jnp.float32, smallest / len(pieces), high / len(pieces)))
        level = level * jnp.repeat(heights, extent[dim] // shards_of).reshape([-1 if axis == dim else 1 for axis in range(len(extent))])
    return level


def rank_bounds(amount, skew):
    portions = [(1 << 20) // math.isqrt(standing ** skew) + 1 for standing in range(1, amount + 1)]
    width = 1 + sum(portions) // (1 << 30)
    return np.cumsum(np.array([max(1, weight // width) for weight in portions]))


def skewed_ids(own_key, extent, count, skew):
    listing = rank_bounds(count, skew)
    ticket = jax.random.randint(jax.random.fold_in(own_key, 1), extent, 0, int(listing[count - 1]))
    grade = jnp.searchsorted(jnp.asarray(listing, jnp.int32), ticket, side="right")
    return jax.random.permutation(jax.random.fold_in(own_key, 2), count)[grade].astype(jnp.int32)


def noise(stream_key, extent, width, most, pieces=(), kind=jnp.bfloat16):
    values = width * jax.random.normal(stream_key, extent, jnp.float32)
    if pieces:
        values = values * levels(stream_key, extent, pieces, -0.22, 0.18)
    return jnp.clip(values, -most, most).astype(kind)


def setup_inputs(seed: int = 0, part: int = 0) -> dict:
    keys = jax.random.split(jax.random.key(seed), 11)
    part_keys = jax.random.split(jax.random.fold_in(keys[10], part), 11)
    return {
        "latent_query_rows": draw_latent_query_rows(jax.random.fold_in(jax.random.fold_in(keys[10], part), 71), part),
        "rotary_query_parts": noise(part_keys[1], (REQUEST_COUNT, LOCAL_HEADS * ROPE), 0.5, 3.0, ((0, 16),)),
        "latent_cache_rows": draw_latent_cache_rows(jax.random.fold_in(jax.random.fold_in(keys[10], part), 71), part),
        "rotary_cache_keys": noise(part_keys[3], (REQUEST_COUNT, ROPE, CACHE), 1.0, 6.0, ((0, 16),)),
        "lengths": draw_lengths(jax.random.fold_in(jax.random.fold_in(keys[10], part), 71), part),
        "adapters": plant(skewed_ids(part_keys[5], (REQUEST_COUNT,), ADAPTER_COUNT, 2), jax.random.fold_in(part_keys[5], 3), 0, ADAPTER_COUNT - 1).astype(jnp.int32),
        "value_up_weight": noise(keys[6], (LOCAL_HEADS, LAT, VALUE_WIDTH), (LAT // 32) ** -0.5, 1.5, ((0, 16),)),
        "output_weight": noise(keys[7], (LOCAL_HEADS * VALUE_WIDTH, MODEL_WIDTH), (LOCAL_HEADS * VALUE_WIDTH) ** -0.5, 0.0625, ((0, 16),)),
        "down_factor_matrix": noise(keys[8], (LOCAL_HEADS * VALUE_WIDTH, ADAPTER_COUNT * ADAPTER_RANK), (LOCAL_HEADS * VALUE_WIDTH) ** -0.5, 0.0625, ((0, 16),)),
        "up_factor_matrix": noise(keys[9], (ADAPTER_RANK, ADAPTER_COUNT, MODEL_WIDTH), ADAPTER_RANK ** -0.5, 1.5, ((0, 16),)),
    }


score_scale = 192.0 ** -0.5


def reference(latent_query_rows, rotary_query_parts, latent_cache_rows, rotary_cache_keys, lengths, adapters, value_up_weight, output_weight, down_factor_matrix, up_factor_matrix):
    query_lat = latent_query_rows.astype(jnp.float32)
    query_pos = rotary_query_parts.reshape(REQUEST_COUNT, LOCAL_HEADS, ROPE).astype(jnp.float32)
    cache_lat = latent_cache_rows.astype(jnp.float32)
    scores = (jnp.einsum("rhl,rtl->rht", query_lat, cache_lat)
              + jnp.einsum("rhp,rpt->rht", query_pos, rotary_cache_keys.astype(jnp.float32))) * score_scale
    live_mask = jnp.arange(CACHE)[None, None, :] < lengths[:, None, None]
    row_max = jnp.max(jnp.where(live_mask, scores, -jnp.inf), axis=-1, keepdims=True)
    exponent = jnp.where(live_mask, jnp.exp(scores - row_max), 0.0)
    row_total = jnp.sum(exponent, axis=-1, keepdims=True)
    weights = (exponent / row_total).astype(jnp.bfloat16)
    attended = jnp.einsum("rht,rtl->rhl", weights.astype(jnp.float32), cache_lat).astype(jnp.bfloat16)
    head_value_output = jnp.einsum("rhl,hlv->rhv", attended.astype(jnp.float32), value_up_weight.astype(jnp.float32))
    head_value_output = head_value_output.astype(jnp.bfloat16).reshape(REQUEST_COUNT, LOCAL_HEADS * VALUE_WIDTH)
    main_term = jnp.dot(head_value_output, output_weight, preferred_element_type=jnp.float32)
    selection_mask = jax.nn.one_hot(adapters, ADAPTER_COUNT, dtype=jnp.bfloat16)
    projected_output = jnp.dot(head_value_output, down_factor_matrix, preferred_element_type=jnp.float32).reshape(REQUEST_COUNT, ADAPTER_COUNT, ADAPTER_RANK)
    low_rank = jnp.sum(selection_mask.astype(jnp.float32)[:, :, None] * projected_output, axis=1).astype(jnp.bfloat16)
    adapter_term = jnp.zeros((REQUEST_COUNT, MODEL_WIDTH), jnp.float32)
    for rank_position_index in range(ADAPTER_RANK):
        selected_adapter = jnp.dot(selection_mask, up_factor_matrix[rank_position_index], preferred_element_type=jnp.float32)
        adapter_term = adapter_term + low_rank[:, rank_position_index:rank_position_index + 1].astype(jnp.float32) * selected_adapter
    return (main_term + adapter_term).astype(jnp.bfloat16)
```

```python
import functools

import jax
import jax.numpy as jnp
from jax import lax
from jax.experimental import pallas as pl
from jax.experimental.pallas import tpu as pltpu
from jax.sharding import PartitionSpec as P

score_scale = 192.0 ** (-0.5)
LANES = 128
F32, BF16 = jnp.float32, jnp.bfloat16


def attention_kernel(
    lengths_ref, adapters_ref, query_ref, rotary_ref, cache_ref, keys_ref, out_ref, rows, attended
):
    req_local = rotary_ref.shape[0]
    heads = query_ref.shape[1]
    rope = keys_ref.shape[1]
    cache_len, latent = cache_ref.shape[1:]
    groups = out_ref.shape[0]
    per_group = heads // groups
    per_step = query_ref.shape[0]
    step = pl.program_id(0)

    @pl.when(step == 0)
    def _():
        for pair in range(heads * rope // LANES):
            slab = rotary_ref[:, pair * LANES : (pair + 1) * LANES].astype(F32)
            for half in range(LANES // rope):
                head = pair * (LANES // rope) + half
                part = slab if half == 0 else pltpu.roll(slab, LANES - half * rope, 1)
                rows[pl.ds(head, req_local, stride=heads), :] = part

    position = lax.broadcasted_iota(jnp.int32, (1, cache_len), 1)
    for own in range(per_step):
        request = step * per_step + own
        cache = cache_ref[own]
        start = pl.multiple_of(request * heads, heads)
        query_pos = rows[pl.ds(start, heads), :][:, :rope].astype(BF16)
        scores = lax.dot_general(
            query_ref[own], cache, (((1,), (1,)), ((), ())), preferred_element_type=F32
        ) + jnp.dot(query_pos, keys_ref[own], preferred_element_type=F32)
        scores = scores * score_scale
        live = position < lengths_ref[request]
        row_max = jnp.max(jnp.where(live, scores, -jnp.inf), axis=-1, keepdims=True)
        exponent = jnp.where(live, jnp.exp(scores - row_max), 0.0)
        row_total = jnp.sum(exponent, axis=-1, keepdims=True)
        weights = (exponent / row_total).astype(BF16)
        mixed = jnp.dot(weights, cache, preferred_element_type=F32)
        for part in range(latent // LANES):
            attended[part, pl.ds(start, heads), :] = mixed[:, part * LANES : (part + 1) * LANES]

    @pl.when(step == pl.num_programs(0) - 1)
    def _():
        for group in range(groups):
            for own in range(per_group):
                picked = pl.ds(group * per_group + own, req_local, stride=heads)
                for part in range(latent // LANES):
                    column = own * latent + part * LANES
                    out_ref[group, :, column : column + LANES] = attended[part, picked, :].astype(
                        BF16
                    )
        row = lax.broadcasted_iota(jnp.int32, (req_local, LANES), 0)
        ids = jnp.zeros((req_local, LANES), jnp.int32)
        for request in range(req_local):
            ids = jnp.where(row == request, adapters_ref[request], ids)
        ids = ids.astype(F32).astype(BF16)
        for group in range(groups):
            out_ref[group, :, per_group * latent :] = ids


def attention(query, rotary, cache, keys, lengths, adapters, groups):
    req_local, heads, latent = query.shape
    rope, cache_len = keys.shape[1:]
    per_step = 2
    width = heads // groups * latent + LANES
    return pl.pallas_call(
        attention_kernel,
        grid=(req_local // per_step,),
        in_specs=[
            pl.BlockSpec(memory_space=pltpu.SMEM),
            pl.BlockSpec(memory_space=pltpu.SMEM),
            pl.BlockSpec((per_step, heads, latent), lambda i: (i, 0, 0)),
            pl.BlockSpec((req_local, heads * rope), lambda i: (0, 0)),
            pl.BlockSpec((per_step, cache_len, latent), lambda i: (i, 0, 0)),
            pl.BlockSpec((per_step, rope, cache_len), lambda i: (i, 0, 0)),
        ],
        out_specs=pl.BlockSpec((groups, req_local, width), lambda i: (0, 0, 0)),
        out_shape=jax.ShapeDtypeStruct((groups, req_local, width), BF16),
        scratch_shapes=[
            pltpu.VMEM((req_local * heads, LANES), F32),
            pltpu.VMEM((latent // LANES, req_local * heads, LANES), F32),
        ],
        compiler_params=pltpu.CompilerParams(vmem_limit_bytes=16 << 20),
        name="attention",
    )(lengths, adapters, query, rotary, cache, keys)


def values_kernel(gathered_ref, up_ref, down_ref, values_ref, low_ref, ids_ref):
    heads, latent, width = up_ref.shape
    all_rows = gathered_ref.shape[0]
    columns = down_ref.shape[1]
    ranks = low_ref.shape[0]
    for head in range(heads):
        values_ref[:, head * width : (head + 1) * width] = jnp.dot(
            gathered_ref[:, head * latent : (head + 1) * latent],
            up_ref[head],
            preferred_element_type=F32,
        ).astype(BF16)
    ids = gathered_ref[:, heads * latent :].astype(F32)
    ids_ref[...] = ids.T[:1]
    projected = jnp.dot(values_ref[...], down_ref[...], preferred_element_type=F32)
    column = lax.broadcasted_iota(jnp.int32, (all_rows, columns), 1)
    picked = jnp.where(column // ranks == ids[:, :1].astype(jnp.int32), projected, 0.0)
    folded = picked[:, :LANES]
    for part in range(1, columns // LANES):
        folded = folded + picked[:, part * LANES : (part + 1) * LANES]
    shift = LANES // 2
    while shift >= ranks:
        folded = folded + pltpu.roll(folded, shift, 1)
        shift //= 2
    low_ref[...] = folded.T[:ranks]


def head_values(gathered, value_up, down, ranks):
    all_rows = gathered.shape[0]
    return pl.pallas_call(
        values_kernel,
        out_shape=(
            jax.ShapeDtypeStruct((all_rows, down.shape[0]), BF16),
            jax.ShapeDtypeStruct((ranks, all_rows), F32),
            jax.ShapeDtypeStruct((1, all_rows), F32),
        ),
        compiler_params=pltpu.CompilerParams(vmem_limit_bytes=16 << 20),
        name="head_values",
    )(gathered, value_up, down)


def project_kernel(values_ref, low_ref, ids_ref, weight_ref, up_ref, out_ref):
    adapter_total = up_ref.shape[0]
    all_rows = values_ref.shape[0]
    low = jnp.sum(low_ref[...], axis=0, keepdims=True)
    adapter = lax.broadcasted_iota(jnp.int32, (adapter_total, all_rows), 0)
    chosen = jnp.where(adapter == ids_ref[...].astype(jnp.int32), low, 0.0).astype(BF16)
    total = jnp.dot(values_ref[...], weight_ref[...], preferred_element_type=F32)
    total = total + lax.dot_general(
        chosen, up_ref[...], (((0,), (0,)), ((), ())), preferred_element_type=F32
    )
    out_ref[...] = total.astype(BF16)


def project(values, low, ids, weight, up):
    all_rows, depth = values.shape
    width = weight.shape[1]
    tile = 1024
    whole = lambda a: pl.BlockSpec(a.shape, lambda i: (0, 0))
    return pl.pallas_call(
        project_kernel,
        grid=(width // tile,),
        in_specs=[
            whole(values),
            whole(low),
            whole(ids),
            pl.BlockSpec((depth, tile), lambda i: (0, i)),
            pl.BlockSpec((up.shape[0], tile), lambda i: (0, i)),
        ],
        out_specs=pl.BlockSpec((all_rows, tile), lambda i: (0, i)),
        out_shape=jax.ShapeDtypeStruct((all_rows, width), BF16),
        compiler_params=pltpu.CompilerParams(vmem_limit_bytes=16 << 20),
        name="project",
    )(values, low, ids, weight, up)


def on_device(
    latent_query_rows,
    rotary_query_parts,
    latent_cache_rows,
    rotary_cache_keys,
    lengths,
    adapters,
    value_up_weight,
    output_weight,
    down_factor_matrix,
    up_factor_matrix,
):
    groups = lax.axis_size("dp")
    exchange = functools.partial(
        lax.all_to_all, axis_name="dp", split_axis=0, concat_axis=0, tiled=True
    )
    adapter_total = up_factor_matrix.shape[1]
    ranks = down_factor_matrix.shape[1] // adapter_total
    message = attention(
        latent_query_rows,
        rotary_query_parts,
        latent_cache_rows,
        rotary_cache_keys,
        lengths,
        adapters,
        groups,
    )
    gathered = exchange(message)
    gathered = gathered.reshape(-1, gathered.shape[-1])
    values, low, ids = head_values(gathered, value_up_weight, down_factor_matrix, ranks)
    low = exchange(low)
    partial = project(values, low, ids, output_weight, up_factor_matrix[0])
    parts = exchange(partial.reshape(groups, -1, partial.shape[-1]))
    return jnp.sum(parts.astype(F32), axis=0).astype(BF16)


def solution(mesh):
    placed = (
        P(("rep", "dp"), None, None),
        P(("rep", "dp"), None),
        P(("rep", "dp"), None, None),
        P(("rep", "dp"), None, None),
        P(("rep", "dp")),
        P(("rep", "dp")),
        P("dp", None, None),
        P("dp", None),
        P("dp", None),
        P("dp", None, None),
    )
    return jax.shard_map(
        on_device, mesh=mesh, in_specs=placed, out_specs=P(("rep", "dp"), None), check_vma=False
    )
```

```python
import functools
import math

import jax
import jax.numpy as jnp
from jax import lax
from jax.experimental import pallas as pl
from jax.experimental.pallas import tpu as pltpu
from jax.sharding import PartitionSpec as P

exponent_scale = 192.0 ** (-0.5) * math.log2(math.e)
LANES = 128
PER_STEP = 4
TILE = 1792
GROUPS = 16
SIDE = 4
F32, BF16 = jnp.float32, jnp.bfloat16


def attention_kernel(
    lengths_ref,
    adapters_ref,
    query_ref,
    rotary_ref,
    cache_ref,
    keys_ref,
    out_ref,
    rows,
    attended,
):
    req_local = rotary_ref.shape[0]
    heads = query_ref.shape[1]
    rope = keys_ref.shape[1]
    cache_len, latent = cache_ref.shape[1:]
    groups = out_ref.shape[0]
    per_group = heads // groups
    per_step = query_ref.shape[0]
    step = pl.program_id(0)
    @pl.when(step == 0)
    def _():
        for pair in range(heads * rope // LANES):
            slab = rotary_ref[:, pair * LANES : (pair + 1) * LANES].astype(F32)
            for half in range(LANES // rope):
                head = pair * (LANES // rope) + half
                part = slab if half == 0 else pltpu.roll(slab, LANES - half * rope, 1)
                rows[pl.ds(head, req_local, stride=heads), :] = part

    position = lax.broadcasted_iota(jnp.int32, (1, cache_len), 1)
    starts = [pl.multiple_of((step * per_step + own) * heads, heads) for own in range(per_step)]
    scores = []
    for own in range(per_step):
        query_pos = rows[pl.ds(starts[own], heads), :][:, :rope].astype(BF16)
        scores.append(
            lax.dot_general(
                query_ref[own], cache_ref[own], (((1,), (1,)), ((), ())), preferred_element_type=F32
            )
            + jnp.dot(query_pos, keys_ref[own], preferred_element_type=F32)
        )
    weights = []
    for own in range(per_step):
        live = position < lengths_ref[step * per_step + own]
        masked = jnp.where(live, scores[own] * exponent_scale, -jnp.inf)
        exponent = jnp.exp2(masked - jnp.max(masked, axis=-1, keepdims=True))
        row_total = jnp.sum(exponent, axis=-1, keepdims=True)
        weights.append((exponent * (1.0 / row_total)).astype(BF16))
    for own in range(per_step):
        mixed = jnp.dot(weights[own], cache_ref[own], preferred_element_type=F32)
        for part in range(latent // LANES):
            attended[part, pl.ds(starts[own], heads), :] = mixed[:, part * LANES : (part + 1) * LANES]

    @pl.when(step == pl.num_programs(0) - 1)
    def _():
        row = lax.broadcasted_iota(jnp.int32, (req_local, LANES), 0)
        ids = jnp.zeros((req_local, LANES), jnp.int32)
        for request in range(req_local):
            ids = jnp.where(row == request, adapters_ref[request], ids)
        ids = ids.astype(F32).astype(BF16)
        for group in range(groups):
            for own in range(per_group):
                picked = pl.ds(group * per_group + own, req_local, stride=heads)
                for part in range(latent // LANES):
                    column = own * latent + part * LANES
                    out_ref[group, :, column : column + LANES] = attended[part, picked, :].astype(
                        BF16
                    )
            out_ref[group, :, per_group * latent :] = ids


def in_hbm(array):
    return pltpu.with_memory_space_constraint(array, pltpu.HBM)


def attention(query, rotary, cache, keys, lengths, adapters):
    req_local, heads, latent = query.shape
    rope, cache_len = keys.shape[1:]
    per_step = PER_STEP
    width = heads // GROUPS * latent + LANES
    return pl.pallas_call(
        attention_kernel,
        grid=(req_local // per_step,),
        in_specs=[
            pl.BlockSpec(memory_space=pltpu.SMEM),
            pl.BlockSpec(memory_space=pltpu.SMEM),
            pl.BlockSpec((per_step, heads, latent), lambda i: (i, 0, 0)),
            pl.BlockSpec((req_local, heads * rope), lambda i: (0, 0)),
            pl.BlockSpec((per_step, cache_len, latent), lambda i: (i, 0, 0)),
            pl.BlockSpec((per_step, rope, cache_len), lambda i: (i, 0, 0)),
        ],
        out_specs=pl.BlockSpec((GROUPS, req_local, width), lambda i: (0, 0, 0)),
        out_shape=jax.ShapeDtypeStruct((GROUPS, req_local, width), BF16),
        scratch_shapes=[
            pltpu.VMEM((req_local * heads, LANES), F32),
            pltpu.VMEM((latent // LANES, req_local * heads, LANES), F32),
        ],
        compiler_params=pltpu.CompilerParams(vmem_limit_bytes=16 << 20),
        name="attention",
    )(*map(in_hbm, (lengths, adapters, query, rotary, cache, keys)))


def class_of(index):
    return (index // SIDE + index % SIDE) % 2


MEMBERS = [[i for i in range(GROUPS) if class_of(i) == which] for which in range(2)]


def across_x(index, core):
    y, x = index // SIDE, index % SIDE
    step = -1 if (x % 2 == 1) == (core == 0) else 1
    return y * SIDE + (x + step) % SIDE


def across_y(index, core):
    y, x = index // SIDE, index % SIDE
    step = -1 if (y % 2 == 1) == (core == 0) else 1
    return (y + step) % SIDE * SIDE + x


def own_class():
    index = lax.axis_index("dp")
    return lax.rem(index // SIDE + lax.rem(index, SIDE), 2)


def own_core():
    return lax.rem(lax.axis_index("rep"), 2)


def by_class(rows):
    each = rows.shape[0] // GROUPS
    return [
        jnp.concatenate([rows[i * each : (i + 1) * each] for i in members], axis=0)
        for members in MEMBERS
    ]


def project_kernel(
    gathered_ref,
    up_ref,
    down_ref,
    weight_ref,
    low_ref,
    ids_ref,
    own_ref,
    first_ref,
    second_ref,
    up,
    down,
    weight,
    values,
    arrived,
):
    tiles = weight.shape[0]
    copies = [
        pltpu.make_async_copy(up_ref, up, arrived.at[0]),
        pltpu.make_async_copy(down_ref, down, arrived.at[1]),
    ] + [
        pltpu.make_async_copy(
            weight_ref.at[:, tile * TILE : (tile + 1) * TILE],
            weight.at[tile],
            arrived.at[2 + tile],
        )
        for tile in range(tiles)
    ]
    for copy in copies[:3]:
        copy.start()
    heads, latent, width = up.shape
    all_rows = gathered_ref.shape[0]
    columns = down.shape[1]
    ranks = GROUPS
    own_rows = all_rows // 2
    parity, core = own_class(), own_core()
    copies[0].wait()
    for copy in copies[3:]:
        copy.start()
    for head in range(heads):
        result = jnp.dot(
            gathered_ref[:, head * latent : (head + 1) * latent],
            up[head],
            preferred_element_type=F32,
        )
        for which, part in enumerate(by_class(result)):
            values[which, :, head * width : (head + 1) * width] = part.astype(BF16)
    ids = jnp.concatenate(by_class(gathered_ref[:, heads * latent :].astype(F32)), axis=0)
    copies[1].wait()
    projected = jnp.dot(
        values[...].reshape(all_rows, heads * width), down[...], preferred_element_type=F32
    )
    column = lax.broadcasted_iota(jnp.int32, (all_rows, columns), 1)
    picked = jnp.where(column // ranks == ids[:, :1].astype(jnp.int32), projected, 0.0)
    folded = picked[:, :LANES]
    for part in range(1, columns // LANES):
        folded = folded + picked[:, part * LANES : (part + 1) * LANES]
    shift = LANES // 2
    while shift >= ranks:
        folded = folded + pltpu.roll(folded, shift, 1)
        shift //= 2
    low = folded.T[:ranks]
    first = (low, pltpu.roll(low, LANES // 2, 1))
    for index in range(GROUPS):
        chosen = first[class_of(index)]
        pair = [chosen[rank : rank + 1] for rank in (across_y(index, 0), across_y(index, 1))]
        low_ref[index, 0:1, :] = chosen[index : index + 1]
        low_ref[index, 1:2, :] = jnp.where(core == 0, *pair)
    ids = ids.T[:8]
    ids_ref[...] = jnp.where(parity == 0, ids, pltpu.roll(ids, LANES // 2, 1))

    ordered = jnp.concatenate([values[1 - parity], values[parity]], axis=0)
    for tile in range(tiles):
        copies[2 + tile].wait()
        total = jnp.dot(ordered, weight[tile], preferred_element_type=F32)
        other_ref = (first_ref, second_ref)[tile // (tiles // 2)]
        part = tile % (tiles // 2)
        other_ref[:, part * TILE : (part + 1) * TILE] = total[:own_rows].astype(BF16)
        own_ref[:, tile * TILE : (tile + 1) * TILE] = total[own_rows:]


def project(gathered, value_up, down, weight):
    in_vmem = pl.BlockSpec(memory_space=pltpu.VMEM)
    rows, (depth, width) = gathered.shape[0], weight.shape
    tiles = width // TILE
    return pl.pallas_call(
        project_kernel,
        in_specs=[in_vmem] + [pl.BlockSpec(memory_space=pl.ANY)] * 3,
        out_specs=[in_vmem] * 5,
        out_shape=[
            jax.ShapeDtypeStruct((GROUPS, 2, LANES), F32),
            jax.ShapeDtypeStruct((8, LANES), F32),
            jax.ShapeDtypeStruct((rows // 2, width), F32),
            jax.ShapeDtypeStruct((rows // 2, width // 2), BF16),
            jax.ShapeDtypeStruct((rows // 2, width // 2), BF16),
        ],
        scratch_shapes=[
            pltpu.VMEM(value_up.shape, BF16),
            pltpu.VMEM(down.shape, BF16),
            pltpu.VMEM((tiles, depth, TILE), BF16),
            pltpu.VMEM((2, rows // 2, depth), BF16),
            pltpu.SemaphoreType.DMA((2 + tiles,)),
        ],
        compiler_params=pltpu.CompilerParams(vmem_limit_bytes=32 << 20),
        name="project",
    )(gathered, *map(in_hbm, (value_up, down, weight)))


def adapt_kernel(
    low_ref,
    ids_ref,
    own_ref,
    up_ref,
    other_up_ref,
    first_ref,
    second_ref,
    out_ref,
    ups,
    own,
    received,
    arrived,
):
    tiles = ups.shape[0]
    adapter_total = up_ref.shape[0]
    own_rows = own_ref.shape[0]
    copies = []
    for tile in range(tiles):
        columns = pl.ds(tile * TILE, TILE)
        here = pl.ds(tile % (tiles // 2) * TILE, TILE)
        received_ref = (first_ref, second_ref)[tile // (tiles // 2)]
        pairs = (
            (up_ref.at[:, columns], ups.at[tile, pl.ds(0, adapter_total)]),
            (other_up_ref.at[:, columns], ups.at[tile, pl.ds(adapter_total, adapter_total)]),
            (own_ref.at[:, columns], own.at[tile]),
            (received_ref.at[:, here], received.at[tile]),
        )
        copies.append(
            [
                pltpu.make_async_copy(source, target, arrived.at[tile, i])
                for i, (source, target) in enumerate(pairs)
            ]
        )
        for copy in copies[-1]:
            copy.start()
    low = jnp.sum(low_ref[...], axis=0)[:, :own_rows]
    adapter = lax.broadcasted_iota(jnp.int32, (adapter_total, own_rows), 0)
    mine = adapter == ids_ref[:1, :own_rows].astype(jnp.int32)
    chosen = jnp.concatenate(
        [jnp.where(mine, low[slot : slot + 1], 0.0) for slot in range(2)], axis=0
    )
    chosen = chosen.T.astype(BF16)
    for tile in range(tiles):
        for copy in copies[tile]:
            copy.wait()
        total = own[tile] + received[tile].astype(F32)
        total = total + jnp.dot(chosen, ups[tile], preferred_element_type=F32)
        out_ref[:, tile * TILE : (tile + 1) * TILE] = total.astype(BF16)


def adapt(low, ids, own, up, other_up, received):
    in_vmem = pl.BlockSpec(memory_space=pltpu.VMEM)
    rows, width = own.shape
    tiles = width // TILE
    return pl.pallas_call(
        adapt_kernel,
        in_specs=[in_vmem] * 2 + [pl.BlockSpec(memory_space=pl.ANY)] * 5,
        out_specs=in_vmem,
        out_shape=jax.ShapeDtypeStruct(own.shape, BF16),
        scratch_shapes=[
            pltpu.VMEM((tiles, 2 * up.shape[0], TILE), BF16),
            pltpu.VMEM((tiles, rows, TILE), F32),
            pltpu.VMEM((tiles, rows, TILE), BF16),
            pltpu.SemaphoreType.DMA((tiles, 4)),
        ],
        compiler_params=pltpu.CompilerParams(vmem_limit_bytes=16 << 20),
        name="adapt",
    )(low, ids, own, in_hbm(up), other_up, *received)


def on_device(
    latent_query_rows,
    rotary_query_parts,
    latent_cache_rows,
    rotary_cache_keys,
    lengths,
    adapters,
    value_up_weight,
    output_weight,
    down_factor_matrix,
    up_factor_matrix,
):
    exchange = functools.partial(
        lax.all_to_all, axis_name="dp", split_axis=0, concat_axis=0, tiled=True
    )
    replicas = lax.axis_size("rep")
    swap = lambda array, partner: lax.ppermute(
        array,
        ("dp", "rep"),
        [
            (index * replicas + rep, partner(index, rep % 2) * replicas + rep)
            for index in range(GROUPS)
            for rep in range(replicas)
        ],
    )
    up = up_factor_matrix[0]
    other_up = swap(up, across_y)
    message = attention(
        latent_query_rows,
        rotary_query_parts,
        latent_cache_rows,
        rotary_cache_keys,
        lengths,
        adapters,
    )
    gathered = exchange(message)
    gathered = gathered.reshape(-1, gathered.shape[-1])
    low, ids, own, *others = project(
        gathered, value_up_weight, down_factor_matrix, output_weight
    )
    received = [
        swap(part, lambda index, _, half=half: across_x(index, half))
        for half, part in enumerate(others)
    ]
    low = exchange(low)
    partial = adapt(low, ids, own, up, other_up, received)
    parts = exchange(
        partial.reshape(GROUPS // 2, -1, partial.shape[-1]), axis_index_groups=MEMBERS
    )
    return jnp.sum(parts.astype(F32), axis=0).astype(BF16)


def solution(mesh):
    placed = (
        P(("rep", "dp"), None, None),
        P(("rep", "dp"), None),
        P(("rep", "dp"), None, None),
        P(("rep", "dp"), None, None),
        P(("rep", "dp")),
        P(("rep", "dp")),
        P("dp", None, None),
        P("dp", None),
        P("dp", None),
        P("dp", None, None),
    )
    return jax.shard_map(
        on_device, mesh=mesh, in_specs=placed, out_specs=P(("rep", "dp"), None), check_vma=False
    )
```

```python
import functools
import math

import jax
import jax.numpy as jnp
from jax import lax
from jax.experimental import pallas as pl
from jax.experimental.pallas import tpu as pltpu
from jax.sharding import PartitionSpec as P

exponent_scale = 192.0 ** (-0.5) * math.log2(math.e)
LANES = 128
PER_STEP = 4
TILE = 1792
GROUPS = 16
SIDE = 4
CLASSES = 4
F32, BF16 = jnp.float32, jnp.bfloat16


def attention_kernel(
    lengths_ref,
    adapters_ref,
    query_ref,
    rotary_ref,
    cache_ref,
    keys_ref,
    weight_in,
    out_ref,
    weight_out,
    rows,
    attended,
    arrived,
):
    staging = pltpu.make_async_copy(weight_in.at[:, :TILE], weight_out, arrived.at[0])
    req_local = rotary_ref.shape[0]
    heads = query_ref.shape[1]
    rope = keys_ref.shape[1]
    cache_len, latent = cache_ref.shape[1:]
    groups = out_ref.shape[0]
    per_group = heads // groups
    per_step = query_ref.shape[0]
    step = pl.program_id(0)
    @pl.when(step == 0)
    def _():
        staging.start()
        for pair in range(heads * rope // LANES):
            slab = rotary_ref[:, pair * LANES : (pair + 1) * LANES].astype(F32)
            for half in range(LANES // rope):
                head = pair * (LANES // rope) + half
                part = slab if half == 0 else pltpu.roll(slab, LANES - half * rope, 1)
                rows[pl.ds(head, req_local, stride=heads), :] = part

    position = lax.broadcasted_iota(jnp.int32, (1, cache_len), 1)
    starts = [pl.multiple_of((step * per_step + own) * heads, heads) for own in range(per_step)]
    scores = []
    for own in range(per_step):
        query_pos = rows[pl.ds(starts[own], heads), :][:, :rope].astype(BF16)
        scores.append(
            lax.dot_general(
                query_ref[own], cache_ref[own], (((1,), (1,)), ((), ())), preferred_element_type=F32
            )
            + jnp.dot(query_pos, keys_ref[own], preferred_element_type=F32)
        )
    weights = []
    for own in range(per_step):
        live = position < lengths_ref[step * per_step + own]
        masked = jnp.where(live, scores[own] * exponent_scale, -jnp.inf)
        exponent = jnp.exp2(masked - jnp.max(masked, axis=-1, keepdims=True))
        row_total = jnp.sum(exponent, axis=-1, keepdims=True)
        weights.append((exponent * (1.0 / row_total)).astype(BF16))
    for own in range(per_step):
        mixed = jnp.dot(weights[own], cache_ref[own], preferred_element_type=F32)
        for part in range(latent // LANES):
            attended[part, pl.ds(starts[own], heads), :] = mixed[:, part * LANES : (part + 1) * LANES]

    @pl.when(step == pl.num_programs(0) - 1)
    def _():
        row = lax.broadcasted_iota(jnp.int32, (req_local, LANES), 0)
        ids = jnp.zeros((req_local, LANES), jnp.int32)
        for request in range(req_local):
            ids = jnp.where(row == request, adapters_ref[request], ids)
        ids = ids.astype(F32).astype(BF16)
        for group in range(groups):
            for own in range(per_group):
                picked = pl.ds(group * per_group + own, req_local, stride=heads)
                for part in range(latent // LANES):
                    column = own * latent + part * LANES
                    out_ref[group, :, column : column + LANES] = attended[part, picked, :].astype(
                        BF16
                    )
            out_ref[group, :, per_group * latent :] = ids
        staging.wait()


def in_hbm(array):
    return pltpu.with_memory_space_constraint(array, pltpu.HBM)


def attention(query, rotary, cache, keys, lengths, adapters, weight):
    req_local, heads, latent = query.shape
    rope, cache_len = keys.shape[1:]
    per_step = PER_STEP
    width = heads // GROUPS * latent + LANES
    anywhere = pl.BlockSpec(memory_space=pl.ANY)
    return pl.pallas_call(
        attention_kernel,
        grid=(req_local // per_step,),
        in_specs=[
            pl.BlockSpec(memory_space=pltpu.SMEM),
            pl.BlockSpec(memory_space=pltpu.SMEM),
            pl.BlockSpec((per_step, heads, latent), lambda i: (i, 0, 0)),
            pl.BlockSpec((req_local, heads * rope), lambda i: (0, 0)),
            pl.BlockSpec((per_step, cache_len, latent), lambda i: (i, 0, 0)),
            pl.BlockSpec((per_step, rope, cache_len), lambda i: (i, 0, 0)),
            anywhere,
        ],
        out_specs=[
            pl.BlockSpec((GROUPS, req_local, width), lambda i: (0, 0, 0)),
            anywhere,
        ],
        out_shape=[
            jax.ShapeDtypeStruct((GROUPS, req_local, width), BF16),
            pltpu.VMEM((weight.shape[0], TILE), BF16),
        ],
        scratch_shapes=[
            pltpu.VMEM((req_local * heads, LANES), F32),
            pltpu.VMEM((latent // LANES, req_local * heads, LANES), F32),
            pltpu.SemaphoreType.DMA((1,)),
        ],
        compiler_params=pltpu.CompilerParams(vmem_limit_bytes=16 << 20),
        name="attention",
    )(*map(in_hbm, (lengths, adapters, query, rotary, cache, keys, weight)))


def class_of(index):
    return (index // SIDE + 2 * (index % SIDE)) % CLASSES


MEMBERS = [[i for i in range(GROUPS) if class_of(i) == which] for which in range(CLASSES)]
PEERS = (2, 9, 11)


def across_x(index, core):
    y, x = index // SIDE, index % SIDE
    step = -1 if (x % 2 == 1) == (core == 0) else 1
    return y * SIDE + (x + step) % SIDE


def along_y(index, step):
    return (index // SIDE + step) % SIDE * SIDE + index % SIDE


def own_place():
    index = lax.axis_index("dp")
    y, x = index // SIDE, lax.rem(index, SIDE)
    return lax.rem(y + 2 * x, CLASSES), 2 * (y // 2) + x // 2


def own_core():
    return lax.rem(lax.axis_index("rep"), 2)


def by_class(rows):
    each = rows.shape[0] // GROUPS
    return [
        jnp.concatenate([rows[i * each : (i + 1) * each] for i in members], axis=0)
        for members in MEMBERS
    ]


def project_kernel(
    gathered_ref,
    first_tile,
    up_ref,
    down_ref,
    weight_ref,
    low_ref,
    ids_ref,
    own_ref,
    above_ref,
    across_ref,
    below_ref,
    up,
    down,
    weight,
    values,
    arrived,
):
    tiles = weight.shape[0] + 1
    copies = [
        pltpu.make_async_copy(up_ref, up, arrived.at[0]),
        pltpu.make_async_copy(down_ref, down, arrived.at[1]),
    ] + [
        pltpu.make_async_copy(
            weight_ref.at[:, tile * TILE : (tile + 1) * TILE],
            weight.at[tile - 1],
            arrived.at[1 + tile],
        )
        for tile in range(1, tiles)
    ]
    for copy in copies:
        copy.start()
    heads, latent, width = up.shape
    all_rows = gathered_ref.shape[0]
    columns = down.shape[1]
    ranks = GROUPS
    own_rows = all_rows // CLASSES
    (which_own, _), core = own_place(), own_core()
    copies[0].wait()
    for head in range(heads):
        result = jnp.dot(
            gathered_ref[:, head * latent : (head + 1) * latent],
            up[head],
            preferred_element_type=F32,
        )
        for which, part in enumerate(by_class(result)):
            values[which, :, head * width : (head + 1) * width] = part.astype(BF16)
    ids = jnp.concatenate(by_class(gathered_ref[:, heads * latent :].astype(F32)), axis=0)
    copies[1].wait()
    projected = jnp.dot(
        values[...].reshape(all_rows, heads * width), down[...], preferred_element_type=F32
    )
    column = lax.broadcasted_iota(jnp.int32, (all_rows, columns), 1)
    picked = jnp.where(column // ranks == ids[:, :1].astype(jnp.int32), projected, 0.0)
    folded = picked[:, :LANES]
    for part in range(1, columns // LANES):
        folded = folded + picked[:, part * LANES : (part + 1) * LANES]
    shift = LANES // 2
    while shift >= ranks:
        folded = folded + pltpu.roll(folded, shift, 1)
        shift //= 2
    low = folded.T[:ranks]
    turns = [(LANES - which * own_rows) % LANES for which in range(CLASSES)]
    turned = [low if turn == 0 else pltpu.roll(low, turn, 1) for turn in turns]
    for index in range(GROUPS):
        chosen = turned[class_of(index)]
        low_ref[index, 0:1, :] = chosen[index : index + 1]
        above, below = along_y(index, 1), along_y(index, -1)
        pairs = ((above, below), (below, above), (across_x(index, 0), across_x(index, 1)))
        for slot, pair in enumerate(pairs):
            pair = [chosen[rank : rank + 1] for rank in pair]
            low_ref[index, slot + 1 : slot + 2, :] = jnp.where(core == 0, *pair)
    ids = ids.T[:8]
    own_ids = ids
    for which in range(1, CLASSES):
        own_ids = jnp.where(which_own == which, pltpu.roll(ids, turns[which], 1), own_ids)
    ids_ref[...] = own_ids

    ordered = jnp.concatenate(
        [values[lax.rem(which_own + step, CLASSES)] for step in (1, 2, 3, 0)], axis=0
    )
    for tile in range(tiles):
        if tile > 0:
            copies[1 + tile].wait()
        part = weight[tile - 1] if tile > 0 else first_tile[...]
        total = jnp.dot(ordered, part, preferred_element_type=F32)
        columns = pl.ds(tile * TILE, TILE)
        for i, other_ref in enumerate((above_ref, across_ref, below_ref)):
            other_ref[:, columns] = total[i * own_rows : (i + 1) * own_rows].astype(BF16)
        own_ref[:, columns] = total[3 * own_rows :]


def project(gathered, first_tile, value_up, down, weight):
    in_vmem = pl.BlockSpec(memory_space=pltpu.VMEM)
    rows, (depth, width) = gathered.shape[0], weight.shape
    tiles = width // TILE
    return pl.pallas_call(
        project_kernel,
        in_specs=[in_vmem] * 2 + [pl.BlockSpec(memory_space=pl.ANY)] * 3,
        out_specs=[in_vmem] * 6,
        out_shape=[
            jax.ShapeDtypeStruct((GROUPS, 4, LANES), F32),
            jax.ShapeDtypeStruct((8, LANES), F32),
            jax.ShapeDtypeStruct((rows // CLASSES, width), F32),
        ]
        + [jax.ShapeDtypeStruct((rows // CLASSES, width), BF16)] * 3,
        scratch_shapes=[
            pltpu.VMEM(value_up.shape, BF16),
            pltpu.VMEM(down.shape, BF16),
            pltpu.VMEM((tiles - 1, depth, TILE), BF16),
            pltpu.VMEM((CLASSES, rows // CLASSES, depth), BF16),
            pltpu.SemaphoreType.DMA((1 + tiles,)),
        ],
        compiler_params=pltpu.CompilerParams(vmem_limit_bytes=32 << 20),
        name="project",
    )(gathered, first_tile, *map(in_hbm, (value_up, down, weight)))


def adapt_kernel(
    low_ref,
    ids_ref,
    own_ref,
    above_ref,
    across_ref,
    below_ref,
    *refs,
):
    up_refs, out_refs, (ups, totals, arrived) = refs[:4], refs[4:8], refs[8:]
    tiles = ups.shape[0]
    own_rows = own_ref.shape[0]
    adapter_total = up_refs[0].shape[0]
    copies = []
    for tile in range(tiles):
        for slot, up_ref in enumerate(up_refs):
            copies.append(
                pltpu.make_async_copy(
                    up_ref.at[:, tile * TILE : (tile + 1) * TILE],
                    ups.at[tile, pl.ds(slot * adapter_total, adapter_total)],
                    arrived.at[tile, slot],
                )
            )
            copies[-1].start()
    low = jnp.sum(low_ref[...], axis=0)[:, :own_rows]
    adapter = lax.broadcasted_iota(jnp.int32, (adapter_total, own_rows), 0)
    mine = adapter == ids_ref[:1, :own_rows].astype(jnp.int32)
    chosen = jnp.concatenate(
        [jnp.where(mine, low[slot : slot + 1], 0.0) for slot in range(4)], axis=0
    )
    chosen = chosen.T.astype(BF16)
    _, place = own_place()
    each = own_rows // CLASSES
    for tile in range(tiles):
        columns = pl.ds(tile * TILE, TILE)
        total = own_ref[:, columns]
        for received_ref in (above_ref, across_ref, below_ref):
            total = total + received_ref[:, columns].astype(F32)
        for copy in copies[4 * tile : 4 * tile + 4]:
            copy.wait()
        total = total + jnp.dot(chosen, ups[tile], preferred_element_type=F32)
        totals[...] = total.reshape(CLASSES, each, TILE)
        for turn, out_ref in enumerate(out_refs):
            out_ref[:, columns] = totals[place ^ turn].astype(BF16)


def adapt(low, ids, own, received, ups):
    in_vmem = pl.BlockSpec(memory_space=pltpu.VMEM)
    near = [pltpu.with_memory_space_constraint(a, pltpu.VMEM) for a in (own, *received)]
    rows, width = own.shape
    tiles = width // TILE
    return pl.pallas_call(
        adapt_kernel,
        in_specs=[in_vmem] * 6 + [pl.BlockSpec(memory_space=pl.ANY)] * 4,
        out_specs=[in_vmem] * 4,
        out_shape=[jax.ShapeDtypeStruct((rows // CLASSES, width), BF16)] * 4,
        scratch_shapes=[
            pltpu.VMEM((tiles, 4 * ups[0].shape[0], TILE), BF16),
            pltpu.VMEM((CLASSES, rows // CLASSES, TILE), F32),
            pltpu.SemaphoreType.DMA((tiles, 4)),
        ],
        compiler_params=pltpu.CompilerParams(vmem_limit_bytes=16 << 20),
        name="adapt",
    )(low, ids, *near, in_hbm(ups[0]), *ups[1:])


def on_device(
    latent_query_rows,
    rotary_query_parts,
    latent_cache_rows,
    rotary_cache_keys,
    lengths,
    adapters,
    value_up_weight,
    output_weight,
    down_factor_matrix,
    up_factor_matrix,
):
    exchange = functools.partial(
        lax.all_to_all, axis_name="dp", split_axis=0, concat_axis=0, tiled=True
    )
    replicas = lax.axis_size("rep")

    def swap(array, partner):
        pairs = [
            (index * replicas + rep, partner(index, rep))
            for index in range(GROUPS)
            for rep in range(replicas)
        ]
        perm = [(source, index * replicas + rep) for source, (index, rep) in pairs]
        return lax.ppermute(array, ("dp", "rep"), perm)

    to_above = lambda index, rep: (along_y(index, 1), rep)
    to_below = lambda index, rep: (along_y(index, -1), rep)
    to_across = lambda index, rep: (across_x(index, rep % 2), rep)
    up = up_factor_matrix[0]
    up_y = swap(up, lambda index, rep: (along_y(index, 1 if rep % 2 else -1), rep))
    up_x = swap(up, to_across)
    up_other_y = swap(up_y, lambda index, rep: (index, rep ^ 1))
    message, first_tile = attention(
        latent_query_rows,
        rotary_query_parts,
        latent_cache_rows,
        rotary_cache_keys,
        lengths,
        adapters,
        output_weight,
    )
    gathered = exchange(message)
    gathered = gathered.reshape(-1, gathered.shape[-1])
    low, ids, own, *others = project(
        gathered, first_tile, value_up_weight, down_factor_matrix, output_weight
    )
    received = [
        swap(part, partner)
        for part, partner in zip(others, (to_above, to_across, to_below), strict=True)
    ]
    low = exchange(low)
    total, *parts = adapt(low, ids, own, received, (up, up_y, up_other_y, up_x))
    total = total.astype(F32)
    for part, bits in zip(parts, PEERS, strict=True):
        part = lax.ppermute(part, "dp", [(i, i ^ bits) for i in range(GROUPS)])
        total = total + part.astype(F32)
    return total.astype(BF16)


def solution(mesh):
    placed = (
        P(("rep", "dp"), None, None),
        P(("rep", "dp"), None),
        P(("rep", "dp"), None, None),
        P(("rep", "dp"), None, None),
        P(("rep", "dp")),
        P(("rep", "dp")),
        P("dp", None, None),
        P("dp", None),
        P("dp", None),
        P("dp", None, None),
    )
    return jax.shard_map(
        on_device, mesh=mesh, in_specs=placed, out_specs=P(("rep", "dp"), None), check_vma=False
    )
```

```python
import functools
import math

import jax
import jax.numpy as jnp
from jax import lax
from jax.experimental import pallas as pl
from jax.experimental.pallas import tpu as pltpu
from jax.sharding import PartitionSpec as P

exponent_scale = 192.0 ** (-0.5) * math.log2(math.e)
LANES = 128
PER_STEP = 4
TILE = 1792
WIDE = 3584
GROUPS = 16
SIDE = 4
CLASSES = 4
F32, BF16 = jnp.float32, jnp.bfloat16


def attention_kernel(
    lengths_ref,
    adapters_ref,
    query_ref,
    rotary_ref,
    cache_ref,
    keys_ref,
    weight_in,
    out_ref,
    weight_out,
    rows,
    attended,
    arrived,
):
    staging = pltpu.make_async_copy(weight_in.at[:, :TILE], weight_out, arrived.at[0])
    req_local = rotary_ref.shape[0]
    heads = query_ref.shape[1]
    rope = keys_ref.shape[1]
    cache_len, latent = cache_ref.shape[1:]
    groups = out_ref.shape[0]
    per_group = heads // groups
    per_step = query_ref.shape[0]
    step = pl.program_id(0)
    @pl.when(step == 0)
    def _():
        staging.start()
        for pair in range(heads * rope // LANES):
            slab = rotary_ref[:, pair * LANES : (pair + 1) * LANES].astype(F32)
            for half in range(LANES // rope):
                head = pair * (LANES // rope) + half
                part = slab if half == 0 else pltpu.roll(slab, LANES - half * rope, 1)
                rows[pl.ds(head, req_local, stride=heads), :] = part

    position = lax.broadcasted_iota(jnp.int32, (1, cache_len), 1)
    starts = [pl.multiple_of((step * per_step + own) * heads, heads) for own in range(per_step)]
    scores = []
    for own in range(per_step):
        query_pos = rows[pl.ds(starts[own], heads), :][:, :rope].astype(BF16)
        scores.append(
            lax.dot_general(
                query_ref[own], cache_ref[own], (((1,), (1,)), ((), ())), preferred_element_type=F32
            )
            + jnp.dot(query_pos, keys_ref[own], preferred_element_type=F32)
        )
    weights = []
    for own in range(per_step):
        live = position < lengths_ref[step * per_step + own]
        masked = jnp.where(live, scores[own] * exponent_scale, -jnp.inf)
        exponent = jnp.exp2(masked - jnp.max(masked, axis=-1, keepdims=True))
        row_total = jnp.sum(exponent, axis=-1, keepdims=True)
        weights.append((exponent * (1.0 / row_total)).astype(BF16))
    for own in range(per_step):
        mixed = jnp.dot(weights[own], cache_ref[own], preferred_element_type=F32)
        for part in range(latent // LANES):
            attended[part, pl.ds(starts[own], heads), :] = mixed[:, part * LANES : (part + 1) * LANES]

    @pl.when(step == pl.num_programs(0) - 1)
    def _():
        row = lax.broadcasted_iota(jnp.int32, (req_local, LANES), 0)
        ids = jnp.zeros((req_local, LANES), jnp.int32)
        for request in range(req_local):
            ids = jnp.where(row == request, adapters_ref[request], ids)
        ids = ids.astype(F32).astype(BF16)
        for group in range(groups):
            for own in range(per_group):
                picked = pl.ds(group * per_group + own, req_local, stride=heads)
                for part in range(latent // LANES):
                    column = own * latent + part * LANES
                    out_ref[group, :, column : column + LANES] = attended[part, picked, :].astype(
                        BF16
                    )
            out_ref[group, :, per_group * latent :] = ids
        staging.wait()


def in_hbm(array):
    return pltpu.with_memory_space_constraint(array, pltpu.HBM)


def attention(query, rotary, cache, keys, lengths, adapters, weight):
    req_local, heads, latent = query.shape
    rope, cache_len = keys.shape[1:]
    per_step = PER_STEP
    width = heads // GROUPS * latent + LANES
    anywhere = pl.BlockSpec(memory_space=pl.ANY)
    return pl.pallas_call(
        attention_kernel,
        grid=(req_local // per_step,),
        in_specs=[
            pl.BlockSpec(memory_space=pltpu.SMEM),
            pl.BlockSpec(memory_space=pltpu.SMEM),
            pl.BlockSpec((per_step, heads, latent), lambda i: (i, 0, 0)),
            pl.BlockSpec((req_local, heads * rope), lambda i: (0, 0)),
            pl.BlockSpec((per_step, cache_len, latent), lambda i: (i, 0, 0)),
            pl.BlockSpec((per_step, rope, cache_len), lambda i: (i, 0, 0)),
            anywhere,
        ],
        out_specs=[
            pl.BlockSpec((GROUPS, req_local, width), lambda i: (0, 0, 0)),
            anywhere,
        ],
        out_shape=[
            jax.ShapeDtypeStruct((GROUPS, req_local, width), BF16),
            pltpu.VMEM((weight.shape[0], TILE), BF16),
        ],
        scratch_shapes=[
            pltpu.VMEM((req_local * heads, LANES), F32),
            pltpu.VMEM((latent // LANES, req_local * heads, LANES), F32),
            pltpu.SemaphoreType.DMA((1,)),
        ],
        compiler_params=pltpu.CompilerParams(vmem_limit_bytes=16 << 20),
        name="attention",
    )(*map(in_hbm, (lengths, adapters, query, rotary, cache, keys, weight)))


def class_of(index):
    return (index // SIDE + 2 * (index % SIDE)) % CLASSES


MEMBERS = [[i for i in range(GROUPS) if class_of(i) == which] for which in range(CLASSES)]
PEERS = (9, 11, 2)


def across_x(index, core):
    y, x = index // SIDE, index % SIDE
    step = -1 if (x % 2 == 1) == (core == 0) else 1
    return y * SIDE + (x + step) % SIDE


def along_y(index, step):
    return (index // SIDE + step) % SIDE * SIDE + index % SIDE


def own_place():
    index = lax.axis_index("dp")
    y, x = index // SIDE, lax.rem(index, SIDE)
    return lax.rem(y + 2 * x, CLASSES), 2 * (y // 2) + x // 2


def own_core():
    return lax.rem(lax.axis_index("rep"), 2)


def by_class(rows):
    each = rows.shape[0] // GROUPS
    return [
        jnp.concatenate([rows[i * each : (i + 1) * each] for i in members], axis=0)
        for members in MEMBERS
    ]


def project_kernel(
    gathered_ref,
    first_tile,
    up_ref,
    down_ref,
    weight_ref,
    low_ref,
    ids_ref,
    own_ref,
    above_ref,
    below_ref,
    across_ref,
    up,
    down,
    weight,
    values,
    arrived,
):
    tiles = weight.shape[0] + 1
    copies = [
        pltpu.make_async_copy(up_ref, up, arrived.at[0]),
        pltpu.make_async_copy(down_ref, down, arrived.at[1]),
    ] + [
        pltpu.make_async_copy(
            weight_ref.at[:, tile * TILE : (tile + 1) * TILE],
            weight.at[tile - 1],
            arrived.at[1 + tile],
        )
        for tile in range(1, tiles)
    ]
    for copy in copies:
        copy.start()
    heads, latent, width = up.shape
    all_rows = gathered_ref.shape[0]
    columns = down.shape[1]
    ranks = GROUPS
    own_rows = all_rows // CLASSES
    (which_own, _), core = own_place(), own_core()
    copies[0].wait()
    for head in range(heads):
        result = jnp.dot(
            gathered_ref[:, head * latent : (head + 1) * latent],
            up[head],
            preferred_element_type=F32,
        )
        for which, part in enumerate(by_class(result)):
            values[which, :, head * width : (head + 1) * width] = part.astype(BF16)
    ids = jnp.concatenate(by_class(gathered_ref[:, heads * latent :].astype(F32)), axis=0)
    copies[1].wait()
    projected = jnp.dot(
        values[...].reshape(all_rows, heads * width), down[...], preferred_element_type=F32
    )
    column = lax.broadcasted_iota(jnp.int32, (all_rows, columns), 1)
    picked = jnp.where(column // ranks == ids[:, :1].astype(jnp.int32), projected, 0.0)
    folded = picked[:, :LANES]
    for part in range(1, columns // LANES):
        folded = folded + picked[:, part * LANES : (part + 1) * LANES]
    shift = LANES // 2
    while shift >= ranks:
        folded = folded + pltpu.roll(folded, shift, 1)
        shift //= 2
    low = folded.T[:ranks]
    turns = [(LANES - which * own_rows) % LANES for which in range(CLASSES)]
    turned = [low if turn == 0 else pltpu.roll(low, turn, 1) for turn in turns]
    for index in range(GROUPS):
        chosen = turned[class_of(index)]
        low_ref[index, 0:1, :] = chosen[index : index + 1]
        above, below = along_y(index, 1), along_y(index, -1)
        pairs = ((below, above), (above, below), (across_x(index, 0), across_x(index, 1)))
        for slot, pair in enumerate(pairs):
            pair = [chosen[rank : rank + 1] for rank in pair]
            low_ref[index, slot + 1 : slot + 2, :] = jnp.where(core == 0, *pair)
    ids = ids.T[:8]
    own_ids = ids
    for which in range(1, CLASSES):
        own_ids = jnp.where(which_own == which, pltpu.roll(ids, turns[which], 1), own_ids)
    ids_ref[...] = own_ids

    ordered = jnp.concatenate(
        [values[lax.rem(which_own + step, CLASSES)] for step in (1, 3, 2, 0)], axis=0
    )
    for tile in range(tiles):
        if tile > 0:
            copies[1 + tile].wait()
        part = weight[tile - 1] if tile > 0 else first_tile[...]
        total = jnp.dot(ordered, part, preferred_element_type=F32)
        columns = pl.ds(tile * TILE, TILE)
        for i, other_ref in enumerate((above_ref, below_ref, across_ref)):
            other_ref[:, columns] = total[i * own_rows : (i + 1) * own_rows].astype(BF16)
        own_ref[:, columns] = total[3 * own_rows :]


def project(gathered, first_tile, value_up, down, weight):
    in_vmem = pl.BlockSpec(memory_space=pltpu.VMEM)
    rows, (depth, width) = gathered.shape[0], weight.shape
    tiles = width // TILE
    return pl.pallas_call(
        project_kernel,
        in_specs=[in_vmem] * 2 + [pl.BlockSpec(memory_space=pl.ANY)] * 3,
        out_specs=[in_vmem] * 6,
        out_shape=[
            jax.ShapeDtypeStruct((GROUPS, 4, LANES), F32),
            jax.ShapeDtypeStruct((8, LANES), F32),
            jax.ShapeDtypeStruct((rows // CLASSES, width), F32),
        ]
        + [jax.ShapeDtypeStruct((rows // CLASSES, width), BF16)] * 3,
        scratch_shapes=[
            pltpu.VMEM(value_up.shape, BF16),
            pltpu.VMEM(down.shape, BF16),
            pltpu.VMEM((tiles - 1, depth, TILE), BF16),
            pltpu.VMEM((CLASSES, rows // CLASSES, depth), BF16),
            pltpu.SemaphoreType.DMA((1 + tiles,)),
        ],
        compiler_params=pltpu.CompilerParams(vmem_limit_bytes=32 << 20),
        name="project",
    )(gathered, first_tile, *map(in_hbm, (value_up, down, weight)))


def adapt_kernel(
    low_ref,
    ids_ref,
    own_ref,
    above_ref,
    below_ref,
    across_ref,
    *refs,
):
    up_refs, out_refs, (ups, totals, arrived) = refs[:4], refs[4:8], refs[8:]
    tiles = ups.shape[0]
    own_rows = own_ref.shape[0]
    adapter_total = up_refs[0].shape[0]
    copies = []
    for tile in range(tiles):
        for slot, up_ref in enumerate(up_refs):
            copies.append(
                pltpu.make_async_copy(
                    up_ref.at[:, tile * WIDE : (tile + 1) * WIDE],
                    ups.at[tile, pl.ds(slot * adapter_total, adapter_total)],
                    arrived.at[tile, slot],
                )
            )
            copies[-1].start()
    low = jnp.sum(low_ref[...], axis=0)[:, :own_rows]
    adapter = lax.broadcasted_iota(jnp.int32, (adapter_total, own_rows), 0)
    mine = adapter == ids_ref[:1, :own_rows].astype(jnp.int32)
    chosen = jnp.concatenate(
        [jnp.where(mine, low[slot : slot + 1], 0.0) for slot in range(4)], axis=0
    )
    chosen = chosen.T.astype(BF16)
    _, place = own_place()
    each = own_rows // CLASSES
    for tile in range(tiles):
        columns = pl.ds(tile * WIDE, WIDE)
        total = own_ref[:, columns]
        for received_ref in (above_ref, below_ref, across_ref):
            total = total + received_ref[:, columns].astype(F32)
        for copy in copies[4 * tile : 4 * tile + 4]:
            copy.wait()
        total = total + jnp.dot(chosen, ups[tile], preferred_element_type=F32)
        totals[...] = total.reshape(CLASSES, each, WIDE)
        for turn, out_ref in zip((0, 2, 3, 1), out_refs, strict=True):
            out_ref[:, columns] = totals[place ^ turn].astype(BF16)


def adapt(low, ids, own, received, ups):
    in_vmem = pl.BlockSpec(memory_space=pltpu.VMEM)
    near = [pltpu.with_memory_space_constraint(a, pltpu.VMEM) for a in (own, *received)]
    rows, width = own.shape
    tiles = width // WIDE
    return pl.pallas_call(
        adapt_kernel,
        in_specs=[in_vmem] * 6 + [pl.BlockSpec(memory_space=pl.ANY)] * 4,
        out_specs=[in_vmem] * 4,
        out_shape=[jax.ShapeDtypeStruct((rows // CLASSES, width), BF16)] * 4,
        scratch_shapes=[
            pltpu.VMEM((tiles, 4 * ups[0].shape[0], WIDE), BF16),
            pltpu.VMEM((CLASSES, rows // CLASSES, WIDE), F32),
            pltpu.SemaphoreType.DMA((tiles, 4)),
        ],
        compiler_params=pltpu.CompilerParams(vmem_limit_bytes=16 << 20),
        name="adapt",
    )(low, ids, *near, in_hbm(ups[0]), *ups[1:])


def on_device(
    latent_query_rows,
    rotary_query_parts,
    latent_cache_rows,
    rotary_cache_keys,
    lengths,
    adapters,
    value_up_weight,
    output_weight,
    down_factor_matrix,
    up_factor_matrix,
):
    exchange = functools.partial(
        lax.all_to_all, axis_name="dp", split_axis=0, concat_axis=0, tiled=True
    )
    replicas = lax.axis_size("rep")

    def swap(array, partner):
        pairs = [
            (index * replicas + rep, partner(index, rep))
            for index in range(GROUPS)
            for rep in range(replicas)
        ]
        perm = [(source, index * replicas + rep) for source, (index, rep) in pairs]
        return lax.ppermute(array, ("dp", "rep"), perm)

    to_above = lambda index, rep: (along_y(index, 1), rep)
    to_below = lambda index, rep: (along_y(index, -1), rep)
    to_across = lambda index, rep: (across_x(index, rep % 2), rep)
    up = up_factor_matrix[0]
    up_y = swap(up, lambda index, rep: (along_y(index, -1 if rep % 2 else 1), rep))
    up_x = swap(up, to_across)
    up_other_y = swap(up_y, lambda index, rep: (index, rep ^ 1))
    message, first_tile = attention(
        latent_query_rows,
        rotary_query_parts,
        latent_cache_rows,
        rotary_cache_keys,
        lengths,
        adapters,
        output_weight,
    )
    gathered = exchange(message)
    gathered = gathered.reshape(-1, gathered.shape[-1])
    low, ids, own, *others = project(
        gathered, first_tile, value_up_weight, down_factor_matrix, output_weight
    )
    received = [
        swap(part, partner)
        for part, partner in zip(others, (to_above, to_below, to_across), strict=True)
    ]
    low = exchange(low)
    total, *parts = adapt(low, ids, own, received, (up, up_y, up_other_y, up_x))
    total = total.astype(F32)
    for part, bits in zip(parts, PEERS, strict=True):
        part = lax.ppermute(part, "dp", [(i, i ^ bits) for i in range(GROUPS)])
        total = total + part.astype(F32)
    return total.astype(BF16)


def solution(mesh):
    placed = (
        P(("rep", "dp"), None, None),
        P(("rep", "dp"), None),
        P(("rep", "dp"), None, None),
        P(("rep", "dp"), None, None),
        P(("rep", "dp")),
        P(("rep", "dp")),
        P("dp", None, None),
        P("dp", None),
        P("dp", None),
        P("dp", None, None),
    )
    return jax.shard_map(
        on_device, mesh=mesh, in_specs=placed, out_specs=P(("rep", "dp"), None), check_vma=False
    )
```

```python
import functools
import math

import jax
import jax.numpy as jnp
from jax import lax
from jax.experimental import pallas as pl
from jax.experimental.pallas import tpu as pltpu
from jax.sharding import PartitionSpec as P

exponent_scale = 192.0 ** (-0.5) * math.log2(math.e)
LANES = 128
PER_STEP = 4
STAGED = 2816
TILE = 2176
WIDE = 3584
GROUPS = 16
SIDE = 4
CLASSES = 4
F32, BF16 = jnp.float32, jnp.bfloat16


def attention_kernel(
    lengths_ref,
    adapters_ref,
    query_ref,
    rotary_ref,
    cache_ref,
    keys_ref,
    weight_in,
    out_ref,
    weight_out,
    rows,
    attended,
    message,
    arrived,
):
    staging = pltpu.make_async_copy(weight_in.at[:, :STAGED], weight_out, arrived.at[0])
    req_local = rotary_ref.shape[0]
    heads = query_ref.shape[1]
    rope = keys_ref.shape[1]
    cache_len, latent = cache_ref.shape[1:]
    groups = message.shape[0]
    per_group = heads // groups
    per_step = query_ref.shape[0]
    step = pl.program_id(0)
    @pl.when(step == 0)
    def _():
        staging.start()
        for pair in range(heads * rope // LANES):
            slab = rotary_ref[:, pair * LANES : (pair + 1) * LANES].astype(F32)
            for half in range(LANES // rope):
                head = pair * (LANES // rope) + half
                part = slab if half == 0 else pltpu.roll(slab, LANES - half * rope, 1)
                rows[pl.ds(head, req_local, stride=heads), :] = part

    position = lax.broadcasted_iota(jnp.int32, (1, cache_len), 1)
    starts = [pl.multiple_of((step * per_step + own) * heads, heads) for own in range(per_step)]
    scores = []
    for own in range(per_step):
        query_pos = rows[pl.ds(starts[own], heads), :][:, :rope].astype(BF16)
        scores.append(
            lax.dot_general(
                query_ref[own], cache_ref[own], (((1,), (1,)), ((), ())), preferred_element_type=F32
            )
            + jnp.dot(query_pos, keys_ref[own], preferred_element_type=F32)
        )
    weights = []
    for own in range(per_step):
        live = position < lengths_ref[step * per_step + own]
        masked = jnp.where(live, scores[own] * exponent_scale, -jnp.inf)
        exponent = jnp.exp2(masked - jnp.max(masked, axis=-1, keepdims=True))
        row_total = jnp.sum(exponent, axis=-1, keepdims=True)
        weights.append((exponent * (1.0 / row_total)).astype(BF16))
    for own in range(per_step):
        mixed = jnp.dot(weights[own], cache_ref[own], preferred_element_type=F32)
        for part in range(latent // LANES):
            attended[part, pl.ds(starts[own], heads), :] = mixed[:, part * LANES : (part + 1) * LANES]

    @pl.when(step == pl.num_programs(0) - 1)
    def _():
        row = lax.broadcasted_iota(jnp.int32, (req_local, LANES), 0)
        ids = jnp.zeros((req_local, LANES), jnp.int32)
        for request in range(req_local):
            ids = jnp.where(row == request, adapters_ref[request], ids)
        ids = ids.astype(F32).astype(BF16)
        leaving = []
        for group in range(groups):
            for own in range(per_group):
                picked = pl.ds(group * per_group + own, req_local, stride=heads)
                for part in range(latent // LANES):
                    column = own * latent + part * LANES
                    message[group, :, column : column + LANES] = attended[part, picked, :].astype(
                        BF16
                    )
            message[group, :, per_group * latent :] = ids
            if (group + 1) % 4 == 0:
                part = pl.ds(group - 3, 4)
                sent = pltpu.make_async_copy(
                    message.at[part], out_ref.at[part], arrived.at[1 + group // 4]
                )
                sent.start()
                leaving.append(sent)
        for sent in leaving:
            sent.wait()
        staging.wait()


def in_hbm(array):
    return pltpu.with_memory_space_constraint(array, pltpu.HBM)


def attention(query, rotary, cache, keys, lengths, adapters, weight):
    req_local, heads, latent = query.shape
    rope, cache_len = keys.shape[1:]
    per_step = PER_STEP
    width = heads // GROUPS * latent + LANES
    anywhere = pl.BlockSpec(memory_space=pl.ANY)
    return pl.pallas_call(
        attention_kernel,
        grid=(req_local // per_step,),
        in_specs=[
            pl.BlockSpec(memory_space=pltpu.SMEM),
            pl.BlockSpec(memory_space=pltpu.SMEM),
            pl.BlockSpec((per_step, heads, latent), lambda i: (i, 0, 0)),
            pl.BlockSpec((req_local, heads * rope), lambda i: (0, 0)),
            pl.BlockSpec((per_step, cache_len, latent), lambda i: (i, 0, 0)),
            pl.BlockSpec((per_step, rope, cache_len), lambda i: (i, 0, 0)),
            anywhere,
        ],
        out_specs=[
            anywhere,
            anywhere,
        ],
        out_shape=[
            pltpu.HBM((GROUPS, req_local, width), BF16),
            pltpu.VMEM((weight.shape[0], STAGED), BF16),
        ],
        scratch_shapes=[
            pltpu.VMEM((req_local * heads, LANES), F32),
            pltpu.VMEM((latent // LANES, req_local * heads, LANES), F32),
            pltpu.VMEM((GROUPS, req_local, width), BF16),
            pltpu.SemaphoreType.DMA((5,)),
        ],
        compiler_params=pltpu.CompilerParams(vmem_limit_bytes=16 << 20),
        name="attention",
    )(*map(in_hbm, (lengths, adapters, query, rotary, cache, keys, weight)))


def class_of(index):
    return (index // SIDE + 2 * (index % SIDE)) % CLASSES


MEMBERS = [[i for i in range(GROUPS) if class_of(i) == which] for which in range(CLASSES)]
PEERS = (9, 11, 2)
SENDING = ((1, 3, 2), (2, 1, 3))


def across_x(index, core):
    y, x = index // SIDE, index % SIDE
    step = -1 if (x % 2 == 1) == (core == 0) else 1
    return y * SIDE + (x + step) % SIDE


def along_y(index, step):
    return (index // SIDE + step) % SIDE * SIDE + index % SIDE


def own_place():
    index = lax.axis_index("dp")
    y, x = index // SIDE, lax.rem(index, SIDE)
    return lax.rem(y + 2 * x, CLASSES), 2 * (y // 2) + x // 2


def own_core():
    return lax.rem(lax.axis_index("rep"), 2)


def by_class(rows):
    each = rows.shape[0] // GROUPS
    return [
        jnp.concatenate([rows[i * each : (i + 1) * each] for i in members], axis=0)
        for members in MEMBERS
    ]


def project_kernel(
    gathered_ref,
    first_tile,
    up_ref,
    down_ref,
    weight_ref,
    low_ref,
    ids_ref,
    own_ref,
    first_ref,
    second_ref,
    third_ref,
    up,
    down,
    weight,
    values,
    arrived,
):
    tiles = weight.shape[0] + 1
    copies = [
        pltpu.make_async_copy(up_ref, up, arrived.at[0]),
        pltpu.make_async_copy(down_ref, down, arrived.at[1]),
    ] + [
        pltpu.make_async_copy(
            weight_ref.at[:, STAGED + (tile - 1) * TILE : STAGED + tile * TILE],
            weight.at[tile - 1],
            arrived.at[1 + tile],
        )
        for tile in range(1, tiles)
    ]
    for copy in copies:
        copy.start()
    heads, latent, width = up.shape
    all_rows = gathered_ref.shape[0]
    columns = down.shape[1]
    ranks = GROUPS
    own_rows = all_rows // CLASSES
    (which_own, _), core = own_place(), own_core()
    copies[0].wait()
    for head in range(heads):
        result = jnp.dot(
            gathered_ref[:, head * latent : (head + 1) * latent],
            up[head],
            preferred_element_type=F32,
        )
        for which, part in enumerate(by_class(result)):
            values[which, :, head * width : (head + 1) * width] = part.astype(BF16)
    ids = jnp.concatenate(by_class(gathered_ref[:, heads * latent :].astype(F32)), axis=0)
    copies[1].wait()
    projected = jnp.dot(
        values[...].reshape(all_rows, heads * width), down[...], preferred_element_type=F32
    )
    column = lax.broadcasted_iota(jnp.int32, (all_rows, columns), 1)
    picked = jnp.where(column // ranks == ids[:, :1].astype(jnp.int32), projected, 0.0)
    folded = picked[:, :LANES]
    for part in range(1, columns // LANES):
        folded = folded + picked[:, part * LANES : (part + 1) * LANES]
    shift = LANES // 2
    while shift >= ranks:
        folded = folded + pltpu.roll(folded, shift, 1)
        shift //= 2
    low = folded.T[:ranks]
    turns = [(LANES - which * own_rows) % LANES for which in range(CLASSES)]
    turned = [low if turn == 0 else pltpu.roll(low, turn, 1) for turn in turns]
    for index in range(GROUPS):
        chosen = turned[class_of(index)]
        low_ref[index, 0:1, :] = chosen[index : index + 1]
        above, below = along_y(index, 1), along_y(index, -1)
        pairs = ((below, above), (above, below), (across_x(index, 0), across_x(index, 1)))
        for slot, pair in enumerate(pairs):
            pair = [chosen[rank : rank + 1] for rank in pair]
            low_ref[index, slot + 1 : slot + 2, :] = jnp.where(core == 0, *pair)
    ids = ids.T[:8]
    own_ids = ids
    for which in range(1, CLASSES):
        own_ids = jnp.where(which_own == which, pltpu.roll(ids, turns[which], 1), own_ids)
    ids_ref[...] = own_ids

    steps = [jnp.where(core == 0, *pair) for pair in zip(*SENDING, strict=True)] + [0]
    ordered = jnp.concatenate(
        [values[lax.rem(which_own + step, CLASSES)] for step in steps], axis=0
    )
    for tile in range(tiles):
        if tile > 0:
            copies[1 + tile].wait()
        part = weight[tile - 1] if tile > 0 else first_tile[...]
        total = jnp.dot(ordered, part, preferred_element_type=F32)
        columns = pl.ds(0, STAGED) if tile == 0 else pl.ds(STAGED + (tile - 1) * TILE, TILE)
        for i, other_ref in enumerate((first_ref, second_ref, third_ref)):
            other_ref[:, columns] = total[i * own_rows : (i + 1) * own_rows].astype(BF16)
        own_ref[:, columns] = total[3 * own_rows :]


def project(gathered, first_tile, value_up, down, weight):
    in_vmem = pl.BlockSpec(memory_space=pltpu.VMEM)
    rows, (depth, width) = gathered.shape[0], weight.shape
    tiles = 1 + (width - STAGED) // TILE
    return pl.pallas_call(
        project_kernel,
        in_specs=[in_vmem] * 2 + [pl.BlockSpec(memory_space=pl.ANY)] * 3,
        out_specs=[in_vmem] * 6,
        out_shape=[
            jax.ShapeDtypeStruct((GROUPS, 4, LANES), F32),
            jax.ShapeDtypeStruct((8, LANES), F32),
            jax.ShapeDtypeStruct((rows // CLASSES, width), F32),
        ]
        + [jax.ShapeDtypeStruct((rows // CLASSES, width), BF16)] * 3,
        scratch_shapes=[
            pltpu.VMEM(value_up.shape, BF16),
            pltpu.VMEM(down.shape, BF16),
            pltpu.VMEM((tiles - 1, depth, TILE), BF16),
            pltpu.VMEM((CLASSES, rows // CLASSES, depth), BF16),
            pltpu.SemaphoreType.DMA((1 + tiles,)),
        ],
        compiler_params=pltpu.CompilerParams(vmem_limit_bytes=32 << 20),
        name="project",
    )(gathered, first_tile, *map(in_hbm, (value_up, down, weight)))


def adapt_kernel(
    low_ref,
    ids_ref,
    own_ref,
    first_ref,
    second_ref,
    third_ref,
    *refs,
):
    up_refs, out_refs, (ups, totals, arrived) = refs[:4], refs[4:8], refs[8:]
    tiles = ups.shape[0]
    own_rows = own_ref.shape[0]
    adapter_total = up_refs[0].shape[0]
    copies = []
    for tile in range(tiles):
        for slot, up_ref in enumerate(up_refs):
            copies.append(
                pltpu.make_async_copy(
                    up_ref.at[:, tile * WIDE : (tile + 1) * WIDE],
                    ups.at[tile, pl.ds(slot * adapter_total, adapter_total)],
                    arrived.at[tile, slot],
                )
            )
            copies[-1].start()
    low = jnp.sum(low_ref[...], axis=0)[:, :own_rows]
    adapter = lax.broadcasted_iota(jnp.int32, (adapter_total, own_rows), 0)
    mine = adapter == ids_ref[:1, :own_rows].astype(jnp.int32)
    chosen = jnp.concatenate(
        [jnp.where(mine, low[slot : slot + 1], 0.0) for slot in range(4)], axis=0
    )
    chosen = chosen.T.astype(BF16)
    _, place = own_place()
    each = own_rows // CLASSES
    for tile in range(tiles):
        columns = pl.ds(tile * WIDE, WIDE)
        total = own_ref[:, columns]
        for received_ref in (first_ref, second_ref, third_ref):
            total = total + received_ref[:, columns].astype(F32)
        for copy in copies[4 * tile : 4 * tile + 4]:
            copy.wait()
        total = total + jnp.dot(chosen, ups[tile], preferred_element_type=F32)
        totals[...] = total.reshape(CLASSES, each, WIDE)
        for turn, out_ref in zip((0, 2, 3, 1), out_refs, strict=True):
            out_ref[:, columns] = totals[place ^ turn].astype(BF16)


def adapt(low, ids, own, received, ups):
    in_vmem = pl.BlockSpec(memory_space=pltpu.VMEM)
    near = [pltpu.with_memory_space_constraint(a, pltpu.VMEM) for a in (own, *received)]
    rows, width = own.shape
    tiles = width // WIDE
    return pl.pallas_call(
        adapt_kernel,
        in_specs=[in_vmem] * 6 + [pl.BlockSpec(memory_space=pl.ANY)] * 4,
        out_specs=[in_vmem] * 4,
        out_shape=[jax.ShapeDtypeStruct((rows // CLASSES, width), BF16)] * 4,
        scratch_shapes=[
            pltpu.VMEM((tiles, 4 * ups[0].shape[0], WIDE), BF16),
            pltpu.VMEM((CLASSES, rows // CLASSES, WIDE), F32),
            pltpu.SemaphoreType.DMA((tiles, 4)),
        ],
        compiler_params=pltpu.CompilerParams(vmem_limit_bytes=16 << 20),
        name="adapt",
    )(low, ids, *near, in_hbm(ups[0]), *ups[1:])


def on_device(
    latent_query_rows,
    rotary_query_parts,
    latent_cache_rows,
    rotary_cache_keys,
    lengths,
    adapters,
    value_up_weight,
    output_weight,
    down_factor_matrix,
    up_factor_matrix,
):
    exchange = functools.partial(
        lax.all_to_all, axis_name="dp", split_axis=0, concat_axis=0, tiled=True
    )
    replicas = lax.axis_size("rep")

    def swap(array, partner):
        pairs = [
            (index * replicas + rep, partner(index, rep))
            for index in range(GROUPS)
            for rep in range(replicas)
        ]
        perm = [(source, index * replicas + rep) for source, (index, rep) in pairs]
        return lax.ppermute(array, ("dp", "rep"), perm)

    to_above = lambda index, rep: (along_y(index, 1), rep)
    to_below = lambda index, rep: (along_y(index, -1), rep)
    to_across = lambda index, rep: (across_x(index, rep % 2), rep)
    up = up_factor_matrix[0]
    up_y = swap(up, lambda index, rep: (along_y(index, -1 if rep % 2 else 1), rep))
    up_x = swap(up, to_across)
    up_other_y = swap(up_y, lambda index, rep: (index, rep ^ 1))
    message, first_tile = attention(
        latent_query_rows,
        rotary_query_parts,
        latent_cache_rows,
        rotary_cache_keys,
        lengths,
        adapters,
        output_weight,
    )
    gathered = exchange(message)
    gathered = gathered.reshape(-1, gathered.shape[-1])
    low, ids, own, *others = project(
        gathered, first_tile, value_up_weight, down_factor_matrix, output_weight
    )
    ways = {1: to_above, 2: to_across, 3: to_below}
    received = [
        swap(part, lambda index, rep, steps=steps: ways[steps[rep % 2]](index, rep))
        for part, steps in zip(others, zip(*SENDING, strict=True), strict=True)
    ]
    low = exchange(low)
    total, *parts = adapt(low, ids, own, received, (up, up_y, up_other_y, up_x))
    total = total.astype(F32)
    for part, bits in zip(parts, PEERS, strict=True):
        part = lax.ppermute(part, "dp", [(i, i ^ bits) for i in range(GROUPS)])
        total = total + part.astype(F32)
    return total.astype(BF16)


def solution(mesh):
    placed = (
        P(("rep", "dp"), None, None),
        P(("rep", "dp"), None),
        P(("rep", "dp"), None, None),
        P(("rep", "dp"), None, None),
        P(("rep", "dp")),
        P(("rep", "dp")),
        P("dp", None, None),
        P("dp", None),
        P("dp", None),
        P("dp", None, None),
    )
    return jax.shard_map(
        on_device, mesh=mesh, in_specs=placed, out_specs=P(("rep", "dp"), None), check_vma=False
    )
```

```python
import functools
import math

import jax
import jax.numpy as jnp
from jax import lax
from jax.experimental import pallas as pl
from jax.experimental.pallas import tpu as pltpu
from jax.sharding import PartitionSpec as P

exponent_scale = 192.0 ** (-0.5) * math.log2(math.e)
LANES = 128
PER_STEP = 4
STAGED = 2816
TILE = 2176
WIDE = 3584
GROUPS = 16
SIDE = 4
CLASSES = 4
F32, BF16 = jnp.float32, jnp.bfloat16


def attention_kernel(
    lengths_ref,
    adapters_ref,
    query_ref,
    rotary_ref,
    cache_ref,
    keys_ref,
    weight_in,
    out_ref,
    weight_out,
    rows,
    attended,
    message,
    arrived,
):
    staging = pltpu.make_async_copy(weight_in.at[:, :STAGED], weight_out, arrived.at[0])
    req_local = rotary_ref.shape[0]
    heads = query_ref.shape[1]
    rope = keys_ref.shape[1]
    cache_len, latent = cache_ref.shape[1:]
    groups = message.shape[0]
    per_group = heads // groups
    per_step = query_ref.shape[0]
    step = pl.program_id(0)
    @pl.when(step == 0)
    def _():
        staging.start()
        for pair in range(heads * rope // LANES):
            slab = rotary_ref[:, pair * LANES : (pair + 1) * LANES].astype(F32)
            for half in range(LANES // rope):
                head = pair * (LANES // rope) + half
                part = slab if half == 0 else pltpu.roll(slab, LANES - half * rope, 1)
                rows[pl.ds(head, req_local, stride=heads), :] = part

    position = lax.broadcasted_iota(jnp.int32, (1, cache_len), 1)
    starts = [pl.multiple_of((step * per_step + own) * heads, heads) for own in range(per_step)]
    scores = []
    for own in range(per_step):
        query_pos = rows[pl.ds(starts[own], heads), :][:, :rope].astype(BF16)
        scores.append(
            lax.dot_general(
                query_ref[own], cache_ref[own], (((1,), (1,)), ((), ())), preferred_element_type=F32
            )
            + jnp.dot(query_pos, keys_ref[own], preferred_element_type=F32)
        )
    weights = []
    for own in range(per_step):
        live = position < lengths_ref[step * per_step + own]
        masked = jnp.where(live, scores[own] * exponent_scale, -jnp.inf)
        exponent = jnp.exp2(masked - jnp.max(masked, axis=-1, keepdims=True))
        row_total = jnp.sum(exponent, axis=-1, keepdims=True)
        weights.append((exponent * (1.0 / row_total)).astype(BF16))
    for own in range(per_step):
        mixed = jnp.dot(weights[own], cache_ref[own], preferred_element_type=F32)
        for part in range(latent // LANES):
            attended[part, pl.ds(starts[own], heads), :] = mixed[:, part * LANES : (part + 1) * LANES]

    @pl.when(step == pl.num_programs(0) - 1)
    def _():
        row = lax.broadcasted_iota(jnp.int32, (req_local, LANES), 0)
        ids = jnp.zeros((req_local, LANES), jnp.int32)
        for request in range(req_local):
            ids = jnp.where(row == request, adapters_ref[request], ids)
        ids = ids.astype(F32).astype(BF16)
        leaving = []
        for group in range(groups):
            for own in range(per_group):
                picked = pl.ds(group * per_group + own, req_local, stride=heads)
                for part in range(latent // LANES):
                    column = own * latent + part * LANES
                    message[group, :, column : column + LANES] = attended[part, picked, :].astype(
                        BF16
                    )
            message[group, :, per_group * latent :] = ids
            if (group + 1) % 4 == 0:
                part = pl.ds(group - 3, 4)
                sent = pltpu.make_async_copy(
                    message.at[part], out_ref.at[part], arrived.at[1 + group // 4]
                )
                sent.start()
                leaving.append(sent)
        for sent in leaving:
            sent.wait()
        staging.wait()


def in_hbm(array):
    return pltpu.with_memory_space_constraint(array, pltpu.HBM)


def attention(query, rotary, cache, keys, lengths, adapters, weight):
    req_local, heads, latent = query.shape
    rope, cache_len = keys.shape[1:]
    per_step = PER_STEP
    width = heads // GROUPS * latent + LANES
    anywhere = pl.BlockSpec(memory_space=pl.ANY)
    return pl.pallas_call(
        attention_kernel,
        grid=(req_local // per_step,),
        in_specs=[
            pl.BlockSpec(memory_space=pltpu.SMEM),
            pl.BlockSpec(memory_space=pltpu.SMEM),
            pl.BlockSpec((per_step, heads, latent), lambda i: (i, 0, 0)),
            pl.BlockSpec((req_local, heads * rope), lambda i: (0, 0)),
            pl.BlockSpec((per_step, cache_len, latent), lambda i: (i, 0, 0)),
            pl.BlockSpec((per_step, rope, cache_len), lambda i: (i, 0, 0)),
            anywhere,
        ],
        out_specs=[
            anywhere,
            anywhere,
        ],
        out_shape=[
            pltpu.HBM((GROUPS, req_local, width), BF16),
            pltpu.VMEM((weight.shape[0], STAGED), BF16),
        ],
        scratch_shapes=[
            pltpu.VMEM((req_local * heads, LANES), F32),
            pltpu.VMEM((latent // LANES, req_local * heads, LANES), F32),
            pltpu.VMEM((GROUPS, req_local, width), BF16),
            pltpu.SemaphoreType.DMA((5,)),
        ],
        compiler_params=pltpu.CompilerParams(vmem_limit_bytes=16 << 20),
        name="attention",
    )(*map(in_hbm, (lengths, adapters, query, rotary, cache, keys, weight)))


def class_of(index):
    return (index // SIDE + 2 * (index % SIDE)) % CLASSES


MEMBERS = [[i for i in range(GROUPS) if class_of(i) == which] for which in range(CLASSES)]
PEERS = (9, 11, 2)
SENDING = ((1, 3, 2), (2, 1, 3))


def across_x(index, core):
    y, x = index // SIDE, index % SIDE
    step = -1 if (x % 2 == 1) == (core == 0) else 1
    return y * SIDE + (x + step) % SIDE


def along_y(index, step):
    return (index // SIDE + step) % SIDE * SIDE + index % SIDE


def own_place():
    index = lax.axis_index("dp")
    y, x = index // SIDE, lax.rem(index, SIDE)
    return lax.rem(y + 2 * x, CLASSES), 2 * (y // 2) + x // 2


def own_core():
    return lax.rem(lax.axis_index("rep"), 2)


def by_class(rows):
    each = rows.shape[0] // GROUPS
    return [
        jnp.concatenate([rows[i * each : (i + 1) * each] for i in members], axis=0)
        for members in MEMBERS
    ]


def project_kernel(
    gathered_ref,
    first_tile,
    up_ref,
    down_ref,
    weight_ref,
    low_ref,
    ids_ref,
    own_ref,
    first_ref,
    second_ref,
    third_ref,
    up,
    down,
    weight,
    values,
    arrived,
):
    tiles = weight.shape[0] + 1
    copies = [
        pltpu.make_async_copy(up_ref, up, arrived.at[0]),
        pltpu.make_async_copy(down_ref, down, arrived.at[1]),
    ] + [
        pltpu.make_async_copy(
            weight_ref.at[:, STAGED + (tile - 1) * TILE : STAGED + tile * TILE],
            weight.at[tile - 1],
            arrived.at[1 + tile],
        )
        for tile in range(1, tiles)
    ]
    for copy in copies:
        copy.start()
    heads, latent, width = up.shape
    all_rows = gathered_ref.shape[0]
    columns = down.shape[1]
    ranks = GROUPS
    own_rows = all_rows // CLASSES
    (which_own, _), core = own_place(), own_core()
    copies[0].wait()
    for head in range(heads):
        result = jnp.dot(
            gathered_ref[:, head * latent : (head + 1) * latent],
            up[head],
            preferred_element_type=F32,
        )
        for which, part in enumerate(by_class(result)):
            values[which, :, head * width : (head + 1) * width] = part.astype(BF16)
    steps = [jnp.where(core == 0, *pair) for pair in zip(*SENDING, strict=True)] + [0]
    ordered = jnp.concatenate(
        [values[lax.rem(which_own + step, CLASSES)] for step in steps], axis=0
    )

    def multiply(tile):
        if tile > 0:
            copies[1 + tile].wait()
        part = weight[tile - 1] if tile > 0 else first_tile[...]
        total = jnp.dot(ordered, part, preferred_element_type=F32)
        columns = pl.ds(0, STAGED) if tile == 0 else pl.ds(STAGED + (tile - 1) * TILE, TILE)
        for i, other_ref in enumerate((first_ref, second_ref, third_ref)):
            other_ref[:, columns] = total[i * own_rows : (i + 1) * own_rows].astype(BF16)
        own_ref[:, columns] = total[3 * own_rows :]

    multiply(0)
    ids = jnp.concatenate(by_class(gathered_ref[:, heads * latent :].astype(F32)), axis=0)
    copies[1].wait()
    projected = jnp.dot(
        values[...].reshape(all_rows, heads * width), down[...], preferred_element_type=F32
    )
    column = lax.broadcasted_iota(jnp.int32, (all_rows, columns), 1)
    picked = jnp.where(column // ranks == ids[:, :1].astype(jnp.int32), projected, 0.0)
    folded = picked[:, :LANES]
    for part in range(1, columns // LANES):
        folded = folded + picked[:, part * LANES : (part + 1) * LANES]
    shift = LANES // 2
    while shift >= ranks:
        folded = folded + pltpu.roll(folded, shift, 1)
        shift //= 2
    low = folded.T[:ranks]
    turns = [(LANES - which * own_rows) % LANES for which in range(CLASSES)]
    turned = [low if turn == 0 else pltpu.roll(low, turn, 1) for turn in turns]
    for index in range(GROUPS):
        chosen = turned[class_of(index)]
        low_ref[index, 0:1, :] = chosen[index : index + 1]
        above, below = along_y(index, 1), along_y(index, -1)
        pairs = ((below, above), (above, below), (across_x(index, 0), across_x(index, 1)))
        for slot, pair in enumerate(pairs):
            pair = [chosen[rank : rank + 1] for rank in pair]
            low_ref[index, slot + 1 : slot + 2, :] = jnp.where(core == 0, *pair)
    ids = ids.T[:8]
    own_ids = ids
    for which in range(1, CLASSES):
        own_ids = jnp.where(which_own == which, pltpu.roll(ids, turns[which], 1), own_ids)
    ids_ref[...] = own_ids
    for tile in range(1, tiles):
        multiply(tile)


def project(gathered, first_tile, value_up, down, weight):
    in_vmem = pl.BlockSpec(memory_space=pltpu.VMEM)
    rows, (depth, width) = gathered.shape[0], weight.shape
    tiles = 1 + (width - STAGED) // TILE
    return pl.pallas_call(
        project_kernel,
        in_specs=[in_vmem] * 2 + [pl.BlockSpec(memory_space=pl.ANY)] * 3,
        out_specs=[in_vmem] * 6,
        out_shape=[
            jax.ShapeDtypeStruct((GROUPS, 4, LANES), F32),
            jax.ShapeDtypeStruct((8, LANES), F32),
            jax.ShapeDtypeStruct((rows // CLASSES, width), F32),
        ]
        + [jax.ShapeDtypeStruct((rows // CLASSES, width), BF16)] * 3,
        scratch_shapes=[
            pltpu.VMEM(value_up.shape, BF16),
            pltpu.VMEM(down.shape, BF16),
            pltpu.VMEM((tiles - 1, depth, TILE), BF16),
            pltpu.VMEM((CLASSES, rows // CLASSES, depth), BF16),
            pltpu.SemaphoreType.DMA((1 + tiles,)),
        ],
        compiler_params=pltpu.CompilerParams(vmem_limit_bytes=32 << 20),
        name="project",
    )(gathered, first_tile, *map(in_hbm, (value_up, down, weight)))


def adapt_kernel(
    low_ref,
    ids_ref,
    own_ref,
    first_ref,
    second_ref,
    third_ref,
    *refs,
):
    up_refs, out_refs, (ups, totals, arrived) = refs[:4], refs[4:8], refs[8:]
    tiles = ups.shape[0]
    own_rows = own_ref.shape[0]
    adapter_total = up_refs[0].shape[0]
    copies = []
    for tile in range(tiles):
        for slot, up_ref in enumerate(up_refs):
            copies.append(
                pltpu.make_async_copy(
                    up_ref.at[:, tile * WIDE : (tile + 1) * WIDE],
                    ups.at[tile, pl.ds(slot * adapter_total, adapter_total)],
                    arrived.at[tile, slot],
                )
            )
            copies[-1].start()
    low = jnp.sum(low_ref[...], axis=0)[:, :own_rows]
    adapter = lax.broadcasted_iota(jnp.int32, (adapter_total, own_rows), 0)
    mine = adapter == ids_ref[:1, :own_rows].astype(jnp.int32)
    chosen = jnp.concatenate(
        [jnp.where(mine, low[slot : slot + 1], 0.0) for slot in range(4)], axis=0
    )
    chosen = chosen.T.astype(BF16)
    _, place = own_place()
    each = own_rows // CLASSES
    for tile in range(tiles):
        columns = pl.ds(tile * WIDE, WIDE)
        total = own_ref[:, columns]
        for received_ref in (first_ref, second_ref, third_ref):
            total = total + received_ref[:, columns].astype(F32)
        for copy in copies[4 * tile : 4 * tile + 4]:
            copy.wait()
        total = total + jnp.dot(chosen, ups[tile], preferred_element_type=F32)
        totals[...] = total.reshape(CLASSES, each, WIDE)
        for turn, out_ref in zip((0, 2, 3, 1), out_refs, strict=True):
            out_ref[:, columns] = totals[place ^ turn].astype(BF16)


def adapt(low, ids, own, received, ups):
    in_vmem = pl.BlockSpec(memory_space=pltpu.VMEM)
    near = [pltpu.with_memory_space_constraint(a, pltpu.VMEM) for a in (own, *received)]
    rows, width = own.shape
    tiles = width // WIDE
    return pl.pallas_call(
        adapt_kernel,
        in_specs=[in_vmem] * 6 + [pl.BlockSpec(memory_space=pl.ANY)] * 4,
        out_specs=[in_vmem] * 4,
        out_shape=[jax.ShapeDtypeStruct((rows // CLASSES, width), BF16)] * 4,
        scratch_shapes=[
            pltpu.VMEM((tiles, 4 * ups[0].shape[0], WIDE), BF16),
            pltpu.VMEM((CLASSES, rows // CLASSES, WIDE), F32),
            pltpu.SemaphoreType.DMA((tiles, 4)),
        ],
        compiler_params=pltpu.CompilerParams(vmem_limit_bytes=16 << 20),
        name="adapt",
    )(low, ids, *near, in_hbm(ups[0]), *ups[1:])


def on_device(
    latent_query_rows,
    rotary_query_parts,
    latent_cache_rows,
    rotary_cache_keys,
    lengths,
    adapters,
    value_up_weight,
    output_weight,
    down_factor_matrix,
    up_factor_matrix,
):
    exchange = functools.partial(
        lax.all_to_all, axis_name="dp", split_axis=0, concat_axis=0, tiled=True
    )
    replicas = lax.axis_size("rep")

    def swap(array, partner):
        pairs = [
            (index * replicas + rep, partner(index, rep))
            for index in range(GROUPS)
            for rep in range(replicas)
        ]
        perm = [(source, index * replicas + rep) for source, (index, rep) in pairs]
        return lax.ppermute(array, ("dp", "rep"), perm)

    to_above = lambda index, rep: (along_y(index, 1), rep)
    to_below = lambda index, rep: (along_y(index, -1), rep)
    to_across = lambda index, rep: (across_x(index, rep % 2), rep)
    up = up_factor_matrix[0]
    up_y = swap(up, lambda index, rep: (along_y(index, -1 if rep % 2 else 1), rep))
    up_x = swap(up, to_across)
    up_other_y = swap(up_y, lambda index, rep: (index, rep ^ 1))
    message, first_tile = attention(
        latent_query_rows,
        rotary_query_parts,
        latent_cache_rows,
        rotary_cache_keys,
        lengths,
        adapters,
        output_weight,
    )
    gathered = exchange(message)
    gathered = gathered.reshape(-1, gathered.shape[-1])
    low, ids, own, *others = project(
        gathered, first_tile, value_up_weight, down_factor_matrix, output_weight
    )
    ways = {1: to_above, 2: to_across, 3: to_below}
    received = [
        swap(part, lambda index, rep, steps=steps: ways[steps[rep % 2]](index, rep))
        for part, steps in zip(others, zip(*SENDING, strict=True), strict=True)
    ]
    low = exchange(low)
    total, *parts = adapt(low, ids, own, received, (up, up_y, up_other_y, up_x))
    total = total.astype(F32)
    for part, bits in zip(parts, PEERS, strict=True):
        part = lax.ppermute(part, "dp", [(i, i ^ bits) for i in range(GROUPS)])
        total = total + part.astype(F32)
    return total.astype(BF16)


def solution(mesh):
    placed = (
        P(("rep", "dp"), None, None),
        P(("rep", "dp"), None),
        P(("rep", "dp"), None, None),
        P(("rep", "dp"), None, None),
        P(("rep", "dp")),
        P(("rep", "dp")),
        P("dp", None, None),
        P("dp", None),
        P("dp", None),
        P("dp", None, None),
    )
    return jax.shard_map(
        on_device, mesh=mesh, in_specs=placed, out_specs=P(("rep", "dp"), None), check_vma=False
    )
```
